32 devices in a mesh: dp: 8 (over z, y), fsdp: 4 (over x, core).
Axes of the slice: x: 2, y: 2, z: 4, core: 2. Of those that a mesh axis runs over, the one named last changes fastest.
Arguments:
- hidden_in: bfloat16 [4096, 14336], P(('dp', 'fsdp')), may hold values from -6 to 6
- out_grads: bfloat16 [4096, 4096], P(('dp', 'fsdp')), may hold values from -6 to 6
- piece_of: int32 [32, 128], P(('dp', 'fsdp')), may hold values from 0 to 7, never falling along the last dimension, each value on 1 to 32 neighbouring positions
- owner_dp: int32 [32, 8], P(('dp', 'fsdp')), may hold values from 0 to 7, as said below
- owner_slot: int32 [32, 8], P(('dp', 'fsdp')), may hold values from 0 to 3
- sketch_in: bfloat16 [14336, 64], P('fsdp'), may hold values from -0.046875 to 0.046875
- sketch_out: bfloat16 [4096, 64], P('fsdp'), may hold values from -0.09375 to 0.09375
Outputs:
- gram: float32 [192, 4096], P('dp', 'fsdp')
The draws below stay inside these ranges and needn't reach their ends.
Inputs may be any that keep to these rules, and one draw needn't show every extreme that they name: `owner_dp`: each device sends exactly 2 pieces to each of 4 cyclically consecutive dp indices and none to the others; the first of these dp indices is the sender's dp index plus an offset that is the same for all devices that share an fsdp index, modulo 8.
All inputs are finite; a program needn't handle non-finite values.
Results may differ from the reference program's by a relative error of at most 0.0036.
Values may be sent and summed in bfloat16 or wider, within the bound.
No kernel may reach another device: no remote copies, remote signals or barrier semaphores. Data moves between devices by JAX's collectives and lax.ppermute only.
A program may use at most 64 MiB of HBM per device.

```python
import math
import jax
import jax.numpy as jnp
import numpy as np
from jax import lax

D = 4096
FF = 14336
R = 64
CAP = 2
GR = 192
TOK_DEV = 128
PIECES = 8
EX_OWN = 4
EXAMPLES = 128
TOKENS = 4096
N_DP = 8
N_FSDP = 4
DEVICES = 32


def draw_owner_dp(key, part):
    rotate_key, order_key = jax.random.split(jax.random.fold_in(key, 17))
    rotation = jax.random.randint(rotate_key, (N_FSDP,), 0, N_DP).astype(jnp.int32)
    scores = jax.random.randint(order_key, (DEVICES, PIECES), 0, 1 << 20).astype(jnp.int32) * PIECES
    scores = scores + jnp.arange(PIECES, dtype=jnp.int32)[None, :]
    ranking = jnp.argsort(scores, axis=1, stable=True).astype(jnp.int32)
    device_ids = jnp.arange(DEVICES, dtype=jnp.int32)
    column = device_ids % N_FSDP
    group_row = device_ids // N_FSDP
    start_index = (rotation[column] + group_row).astype(jnp.int32)
    shifted = ranking // CAP + start_index[:, None]
    return (shifted % N_DP).astype(jnp.int32)


def set_ends(result, own_key, smallest, high):
    index_at = [jax.random.randint(jax.random.fold_in(own_key, axis), (), 0, length) for axis, length in enumerate(result.shape)]
    widest = result.shape.index(max(result.shape))
    neighbour = index_at[:widest] + [(index_at[widest] + 1) % result.shape[widest]] + index_at[widest + 1:]
    return result.at[tuple(index_at)].set(smallest).at[tuple(neighbour)].set(high)


def shard_levels(rng, shape, pieces, smallest, largest):
    loudness, own = 1.0, jax.random.fold_in(rng, 6)
    for axis_at, shards_of in pieces:
        draws = jnp.exp(jax.random.uniform(jax.random.fold_in(own, axis_at), (shards_of,), jnp.float32, smallest / len(pieces), largest / len(pieces)))
        loudness = loudness * jnp.repeat(draws, shape[axis_at] // shards_of).reshape([-1 if axis == axis_at else 1 for axis in range(len(shape))])
    return loudness


def length_profile(number_of, total, most, skew):
    weights = [(1 << 20) // math.isqrt(rank ** skew) + 1 for rank in range(2, number_of + 1)]
    spare, given = total - most - (number_of - 1), [1] * (number_of - 1)
    while spare > 0:
        movable = [i for i in range(number_of - 1) if given[i] < most]
        whole, left = sum([weights[i] for i in movable]), spare
        for i in movable:
            extra = min(most - given[i], max(1, left * weights[i] // whole), spare)
            given[i] = given[i] + extra
            spare = spare - extra
    return np.array([most] + given)


def ragged_sizes(key, count, total, bound, lean):
    if count == 2:
        one = jax.random.randint(key, (), max(1, total - bound), min(bound, total - 1) + 1)
        return jnp.stack([one, total - one])
    lengths = jnp.asarray(length_profile(count, total, bound, lean), jnp.int32)
    pairs = (count - 1) // 2
    giver, sink = lengths[1:1 + 2 * pairs:2], lengths[2:2 + 2 * pairs:2]
    room = jnp.minimum(giver - 1, bound - sink)
    moved = jax.random.randint(jax.random.fold_in(key, 1), (pairs,), 0, 1 << 20) % (room + 1)
    lengths = lengths.at[1:1 + 2 * pairs:2].set(giver - moved).at[2:2 + 2 * pairs:2].set(sink + moved)
    return lengths[jax.random.permutation(jax.random.fold_in(key, 2), count)]


def noise(key, dims, scale, most, shards=(), held_as=jnp.bfloat16):
    entries = jax.random.normal(key, dims, jnp.float32) * scale
    if len(shards) > 0:
        entries = shard_levels(key, dims, shards, -0.22, 0.18) * entries
    return jnp.clip(entries, min=-most, max=most).astype(held_as)


def setup_inputs(seed: int = 0) -> dict:
    seeds = jax.random.split(jax.random.key(seed), 8)
    hidden_in = noise(seeds[0], (TOKENS, FF), 1.0, 6.0, ((0, 32),))
    out_grads = noise(seeds[1], (TOKENS, D), 1.0, 6.0, ((0, 32),))
    piece_of = jax.vmap(lambda own: jnp.searchsorted(jnp.cumsum(ragged_sizes(own, PIECES, TOK_DEV, 2 * TOK_DEV // PIECES, 1)), jnp.arange(TOK_DEV), side="right"))(jax.random.split(seeds[2], DEVICES)).reshape((DEVICES, TOK_DEV)).astype(jnp.int32)
    owner_dp = draw_owner_dp(jax.random.fold_in(seeds[7], 71), 0)
    owner_slot = set_ends(jax.random.randint(seeds[4], (DEVICES, PIECES), 0, EX_OWN), jax.random.fold_in(seeds[4], 1), 0, EX_OWN - 1).astype(jnp.int32)
    sketch_in = noise(seeds[5], (FF, R), FF ** -0.5, 0.046875, ((0, 4),))
    sketch_out = noise(seeds[6], (D, R), D ** -0.5, 0.09375, ((0, 4),))
    return {"hidden_in": hidden_in, "out_grads": out_grads, "piece_of": piece_of, "owner_dp": owner_dp, "owner_slot": owner_slot, "sketch_in": sketch_in, "sketch_out": sketch_out}


def reference(hidden_in, out_grads, piece_of, owner_dp, owner_slot, sketch_in, sketch_out):
    device_count = N_DP * N_FSDP
    hidden_blocks = hidden_in.reshape(device_count, TOK_DEV, FF)
    grad_blocks = out_grads.reshape(device_count, TOK_DEV, D)

    def project(pack):
        hidden_rows, grad_rows, pieces_row = pack
        inputs_low = jnp.dot(hidden_rows, sketch_in, preferred_element_type=jnp.float32).astype(jnp.bfloat16)
        errors_low = jnp.dot(grad_rows, sketch_out, preferred_element_type=jnp.float32).astype(jnp.bfloat16)
        member = (pieces_row[:, None] == jnp.arange(PIECES, dtype=jnp.int32)[None, :]).astype(jnp.float32)
        outer = jnp.einsum('tp,ti,tj->pij', member, inputs_low.astype(jnp.float32), errors_low.astype(jnp.float32))
        return outer.reshape(PIECES, R * R)
    piece_features = lax.map(project, (hidden_blocks, grad_blocks, piece_of))
    column = (jnp.arange(device_count, dtype=jnp.int32) % N_FSDP).astype(jnp.int32)
    example_key = ((owner_dp * N_FSDP + column[:, None]) * EX_OWN + owner_slot).astype(jnp.int32)
    features = jax.ops.segment_sum(piece_features.reshape(device_count * PIECES, R * R), example_key.reshape(-1), num_segments=EXAMPLES)
    features = features.astype(jnp.bfloat16)
    gram = jnp.dot(features[:, :GR].T, features, preferred_element_type=jnp.float32)
    return gram * (1.0 / math.sqrt(EXAMPLES))
```

```python
import functools
import math

import jax
import jax.numpy as jnp
from jax import lax
from jax.experimental import pallas as pl
from jax.experimental.pallas import tpu as pltpu
from jax.sharding import PartitionSpec as P

CAP = 2
GR = 192
BF16 = jnp.bfloat16
F32 = jnp.float32
KEY_ROWS = 16
CONTRACT_LAST = (((1,), (1,)), ((), ()))
VMEM = pl.BlockSpec(memory_space=pltpu.VMEM)
SMEM = pl.BlockSpec(memory_space=pltpu.SMEM)


def swap(value, axis, bit):
    count = lax.axis_size(axis)
    return lax.ppermute(value, axis, [(i, i ^ bit) for i in range(count)])


def bits_of(count):
    return [1 << k for k in range(count.bit_length() - 1)]


def gather_group(rows):
    bits = bits_of(lax.axis_size("dp"))
    for bit in bits[1:] + bits[:1]:
        rows = jnp.concatenate([rows, swap(rows, "dp", bit)], axis=0)
    return rows


def gather_shards(own):
    shards = {0: own}
    for bit in reversed(bits_of(lax.axis_size("fsdp"))):
        shards.update({k ^ bit: swap(v, "fsdp", bit) for k, v in list(shards.items())})
    return [shards[k] for k in range(len(shards))]


def project_kernel(count, *refs):
    total = refs[2 * count][...] if len(refs) > 2 * count + 1 else 0.0
    for sketch, tokens in zip(refs[:count], refs[count : 2 * count]):
        total += lax.dot_general(
            sketch[...], tokens[...], CONTRACT_LAST, preferred_element_type=F32
        )
    refs[-1][...] = total.astype(refs[-1].dtype)


def project(sketches, tokens, total, dtype):
    operands = [*sketches, *tokens] + ([] if total is None else [total])
    return pl.pallas_call(
        functools.partial(project_kernel, len(sketches)),
        out_shape=jax.ShapeDtypeStruct((sketches[0].shape[0], tokens[0].shape[0]), dtype),
        in_specs=[VMEM] * len(operands),
        out_specs=VMEM,
    )(*operands)


def errors_kernel(count, owned, *refs):
    sketches, tokens = refs[:count], refs[count : 2 * count]
    piece_of, owner_dp, owner_slot, out = refs[2 * count :]
    total = 0.0
    for sketch, part in zip(sketches, tokens):
        total += lax.dot_general(
            sketch[...], part[...], CONTRACT_LAST, preferred_element_type=F32
        )
    width = total.shape[0]
    out[:width, :] = total.astype(BF16)
    piece = piece_of[...]
    key = jnp.zeros(piece.shape, jnp.int32)
    for p in range(owner_dp.shape[1]):
        key = jnp.where(piece == p, owner_dp[0, p] * owned + owner_slot[0, p], key)
    key = jnp.broadcast_to(key.astype(F32), (KEY_ROWS, key.shape[1]))
    out[width:, :] = key.astype(BF16)


def gram_kernel(count_dp, group_examples, scale, *refs):
    groups = len(refs) // 2
    errors, inputs, out = refs[:groups], refs[groups : 2 * groups], refs[-1]
    rows_here, columns_here = out.shape
    width = inputs[0].shape[0] // count_dp
    mine = columns_here // width
    high = width + KEY_ROWS
    start = pl.multiple_of(lax.axis_index("fsdp") * mine, mine)
    place = (rows_here, width)
    column = lax.axis_index("dp") * rows_here + lax.broadcasted_iota(jnp.int32, place, 0)
    at = lax.broadcasted_iota(jnp.int32, place, 1)
    pick_in = (at == column // width).astype(F32).astype(BF16)
    pick_out = (at == column % width).astype(F32).astype(BF16)
    wide, narrow = [], []
    for e_ref, i_ref in zip(errors, inputs):
        err = jnp.concatenate([e_ref[k * high : k * high + width, :] for k in range(count_dp)], axis=1)
        key = jnp.concatenate(
            [e_ref[k * high + width : (k + 1) * high, :] for k in range(count_dp)], axis=1
        )
        key = key.astype(F32)[:1, :]
        low = jnp.concatenate([i_ref[k * width : (k + 1) * width, :] for k in range(count_dp)], axis=1)
        here = jnp.concatenate(
            [i_ref[pl.ds(k * width + start, mine), :] for k in range(count_dp)], axis=1
        )
        example = lax.broadcasted_iota(jnp.int32, (group_examples, key.shape[1]), 0).astype(F32)
        member = (example == key).astype(F32).astype(BF16)
        spread = jnp.concatenate([member * here[i : i + 1, :] for i in range(mine)], axis=0)
        wide.append(
            lax.dot_general(spread, err, CONTRACT_LAST, preferred_element_type=F32).astype(BF16)
        )
        product = jnp.dot(pick_in, low, preferred_element_type=F32) * jnp.dot(
            pick_out, err, preferred_element_type=F32
        )
        upper = product.astype(BF16)
        lower = (product - upper.astype(F32)).astype(BF16)
        part = lax.dot_general(upper, member, CONTRACT_LAST, preferred_element_type=F32)
        part += lax.dot_general(lower, member, CONTRACT_LAST, preferred_element_type=F32)
        narrow.append(part.astype(BF16))
    left = jnp.concatenate(narrow, axis=1)
    blocks = []
    for i in range(mine):
        right = jnp.concatenate(
            [w[i * group_examples : (i + 1) * group_examples, :] for w in wide], axis=0
        )
        blocks.append(jnp.dot(left, right, preferred_element_type=F32))
    out[...] = jnp.concatenate(blocks, axis=1) * scale


def by_tokens(hidden_in, out_grads, piece_of, owner_dp, owner_slot, sketch_in, sketch_out):
    count_dp = lax.axis_size("dp")
    count_fsdp = lax.axis_size("fsdp")
    token_rows = hidden_in.shape[0]
    width = sketch_in.shape[1]
    owned = count_dp // 2
    me = lax.axis_index("fsdp")

    def columns(tokens, k):
        size = tokens.shape[1] // count_fsdp
        return lax.dynamic_slice_in_dim(tokens, (me ^ k) * size, size, axis=1)

    out_shards = gather_shards(sketch_out.T)
    in_shards = gather_shards(sketch_in.T)
    errors = pl.pallas_call(
        functools.partial(errors_kernel, count_fsdp, owned),
        out_shape=jax.ShapeDtypeStruct((width + KEY_ROWS, token_rows), BF16),
        in_specs=[VMEM] * (2 * count_fsdp + 1) + [SMEM] * 2,
        out_specs=VMEM,
    )(
        *out_shards,
        *[columns(out_grads, k) for k in range(count_fsdp)],
        piece_of,
        owner_dp,
        owner_slot,
    )
    near = list(range(max(1, count_fsdp // 2)))
    far = list(range(len(near), count_fsdp))
    inputs = project(
        [in_shards[k] for k in near], [columns(hidden_in, k) for k in near], None, F32
    )
    for k in far:
        inputs = project(
            [in_shards[k]], [columns(hidden_in, k)], inputs, BF16 if k == far[-1] else F32
        )
    all_errors = gather_shards(gather_group(errors))
    all_inputs = gather_shards(gather_group(inputs))
    scale = 1.0 / math.sqrt(owned * count_dp * count_fsdp)
    return pl.pallas_call(
        functools.partial(gram_kernel, count_dp, owned * count_dp, scale),
        out_shape=jax.ShapeDtypeStruct((GR // count_dp, width * width // count_fsdp), F32),
        in_specs=[VMEM] * (2 * count_fsdp),
        out_specs=VMEM,
        compiler_params=pltpu.CompilerParams(vmem_limit_bytes=24 * 1024 * 1024),
    )(*all_errors, *all_inputs)


def by_pieces(hidden_in, out_grads, piece_of, owner_dp, owner_slot, sketch_in, sketch_out):
    count_dp = lax.axis_size("dp")
    count_fsdp = lax.axis_size("fsdp")
    full_in, full_out = (
        lax.all_gather(sketch_in, "fsdp", axis=0, tiled=True),
        lax.all_gather(sketch_out, "fsdp", axis=0, tiled=True),
    )
    inputs_low = jnp.dot(hidden_in, full_in, preferred_element_type=F32).astype(BF16)
    errors_low = jnp.dot(out_grads, full_out, preferred_element_type=F32).astype(BF16)
    rows_here = inputs_low.shape[0]
    width = inputs_low.shape[1]
    pieces = owner_dp.shape[1]
    member = piece_of[0][:, None] == jnp.arange(pieces, dtype=jnp.int32)[None, :]
    spread = (member.astype(BF16)[:, :, None] * inputs_low[:, None, :]).reshape(
        rows_here, pieces * width
    )
    partial_value = lax.dot_general(
        spread, errors_low, (((0,), (0,)), ((), ())), preferred_element_type=F32
    )
    partial_value = partial_value.reshape(pieces, width * width)
    target = owner_dp[0]
    earlier = jnp.arange(pieces)[None, :] < jnp.arange(pieces)[:, None]
    ranked = jnp.sum(((target[:, None] == target[None, :]) & earlier).astype(jnp.int32), axis=1)
    places = target * CAP + ranked
    slots_total = count_dp * CAP
    routing_mask = places[None, :] == jnp.arange(slots_total, dtype=jnp.int32)[:, None]
    outgoing = jnp.dot(routing_mask.astype(F32), partial_value, precision=lax.Precision.HIGHEST)
    labels = jnp.sum(routing_mask.astype(jnp.int32) * (owner_slot[0][None, :] + 1), axis=1) - 1
    incoming, arrived = (
        lax.all_to_all(outgoing, "dp", split_axis=0, concat_axis=0, tiled=True),
        lax.all_to_all(labels, "dp", split_axis=0, concat_axis=0, tiled=True),
    )
    owned = count_dp // 2
    collect = (arrived[None, :] == jnp.arange(owned, dtype=jnp.int32)[:, None]).astype(F32)
    features = jnp.dot(collect, incoming, precision=lax.Precision.HIGHEST).astype(BF16)
    local_gram = lax.dot_general(
        features[:, :GR], features, (((0,), (0,)), ((), ())), preferred_element_type=F32
    )
    scale_factor = 1.0 / math.sqrt(owned * count_dp * count_fsdp)
    section_one = lax.psum_scatter(local_gram, "fsdp", scatter_dimension=1, tiled=True)
    result = lax.psum_scatter(section_one, "dp", scatter_dimension=0, tiled=True)
    return result * scale_factor


def on_device(hidden_in, out_grads, piece_of, owner_dp, owner_slot, sketch_in, sketch_out):
    count_dp = lax.axis_size("dp")
    count_fsdp = lax.axis_size("fsdp")
    token_rows = hidden_in.shape[0]
    width = sketch_in.shape[1]
    gathered = count_dp * count_fsdp * token_rows * 2 * width * 2
    summed = GR * width * width * 4
    doubling = all(n & (n - 1) == 0 for n in (count_dp, count_fsdp))
    whole_tiles = token_rows % 128 == 0 and width % (16 * count_fsdp) == 0
    exact_keys = count_dp * (count_dp // 2) <= 256
    form = by_tokens if gathered <= summed and doubling and whole_tiles and exact_keys else by_pieces
    return form(hidden_in, out_grads, piece_of, owner_dp, owner_slot, sketch_in, sketch_out)


def solution(mesh):
    return jax.shard_map(
        on_device,
        mesh=mesh,
        in_specs=(
            P(("dp", "fsdp"), None),
            P(("dp", "fsdp"), None),
            P(("dp", "fsdp"), None),
            P(("dp", "fsdp"), None),
            P(("dp", "fsdp"), None),
            P("fsdp", None),
            P("fsdp", None),
        ),
        out_specs=P("dp", "fsdp"),
        check_vma=False,
    )
```

```python
import functools
import math

import jax
import jax.numpy as jnp
from jax import lax
from jax.experimental import pallas as pl
from jax.experimental.pallas import tpu as pltpu
from jax.sharding import PartitionSpec as P

CAP = 2
GR = 192
BF16 = jnp.bfloat16
F32 = jnp.float32
KEY_ROWS = 16
CONTRACT_LAST = (((1,), (1,)), ((), ()))
VMEM = pl.BlockSpec(memory_space=pltpu.VMEM)
SMEM = pl.BlockSpec(memory_space=pltpu.SMEM)
ANY = pl.BlockSpec(memory_space=pl.ANY)
ROOM = pltpu.CompilerParams(vmem_limit_bytes=16 * 1024 * 1024)


def swap(value, axis, bit):
    count = lax.axis_size(axis)
    return lax.ppermute(value, axis, [(i, i ^ bit) for i in range(count)])


def bits_of(count):
    return [1 << k for k in range(count.bit_length() - 1)]


def after(value, *others):
    return lax.optimization_barrier((value, *others))[0]


def gather_group(rows):
    bits = bits_of(lax.axis_size("dp"))
    stages = [rows]
    for bit in bits[1:] + bits[:1]:
        rows = jnp.concatenate([rows, swap(rows, "dp", bit)], axis=0)
        stages.append(rows)
    return rows, stages[-2]


def spread(value, bits):
    held = {0: value}
    for bit in reversed(bits):
        held.update({k ^ bit: swap(v, "fsdp", bit) for k, v in list(held.items())})
    return [held[k] for k in range(len(held))]


def low_rank(sketches, which, tokens):
    me = lax.axis_index("fsdp")
    total = 0.0
    for sketch, k in zip(sketches, which):
        size = sketch.shape[1]
        start = pl.multiple_of((me ^ k) * size, size)
        total += lax.dot_general(
            sketch[...], tokens[:, pl.ds(start, size)], CONTRACT_LAST, preferred_element_type=F32
        )
    return total


def project_kernel(which, *refs):
    count = len(which)
    total = low_rank(refs[:count], which, refs[count])
    if len(refs) > count + 2:
        total += refs[count + 1][...]
    refs[-1][...] = total.astype(refs[-1].dtype)


def project(sketches, which, tokens, total, dtype):
    operands = [*sketches, tokens] + ([] if total is None else [total])
    return pl.pallas_call(
        functools.partial(project_kernel, which),
        out_shape=jax.ShapeDtypeStruct((sketches[0].shape[0], tokens.shape[0]), dtype),
        in_specs=[VMEM] * len(operands),
        out_specs=VMEM,
        compiler_params=ROOM,
    )(*operands)


def errors_kernel(which, owned, *refs):
    count = len(which)
    tokens, piece_of, owner_dp, owner_slot, _, out = refs[count:]
    total = low_rank(refs[:count], which, tokens)
    width = total.shape[0]
    out[:width, :] = total.astype(BF16)
    piece = piece_of[...]
    key = jnp.zeros(piece.shape, jnp.int32)
    for p in range(owner_dp.shape[1]):
        key = jnp.where(piece == p, owner_dp[0, p] * owned + owner_slot[0, p], key)
    key = jnp.broadcast_to(key.astype(F32), (KEY_ROWS, key.shape[1]))
    out[width:, :] = key.astype(BF16)


def gram_kernel(count_dp, group_examples, scale, *refs):
    groups = len(refs) // 2
    errors, inputs, out = refs[:groups], refs[groups : 2 * groups], refs[-1]
    rows_here, columns_here = out.shape
    width = inputs[0].shape[0] // count_dp
    mine = columns_here // width
    high = width + KEY_ROWS
    start = pl.multiple_of(lax.axis_index("fsdp") * mine, mine)
    place = (rows_here, width)
    column = lax.axis_index("dp") * rows_here + lax.broadcasted_iota(jnp.int32, place, 0)
    at = lax.broadcasted_iota(jnp.int32, place, 1)
    pick_in = (at == column // width).astype(F32).astype(BF16)
    pick_out = (at == column % width).astype(F32).astype(BF16)
    wide, narrow = [], []
    for e_ref, i_ref in zip(errors, inputs):
        err = jnp.concatenate([e_ref[k * high : k * high + width, :] for k in range(count_dp)], axis=1)
        key = jnp.concatenate(
            [e_ref[k * high + width : (k + 1) * high, :] for k in range(count_dp)], axis=1
        )
        key = key.astype(F32)[:1, :]
        low = jnp.concatenate([i_ref[k * width : (k + 1) * width, :] for k in range(count_dp)], axis=1)
        here = jnp.concatenate(
            [i_ref[pl.ds(k * width + start, mine), :] for k in range(count_dp)], axis=1
        )
        example = lax.broadcasted_iota(jnp.int32, (group_examples, key.shape[1]), 0).astype(F32)
        member = (example == key).astype(F32).astype(BF16)
        spread = jnp.concatenate([member * here[i : i + 1, :] for i in range(mine)], axis=0)
        wide.append(
            lax.dot_general(spread, err, CONTRACT_LAST, preferred_element_type=F32).astype(BF16)
        )
        product = jnp.dot(pick_in, low, preferred_element_type=F32) * jnp.dot(
            pick_out, err, preferred_element_type=F32
        )
        upper = product.astype(BF16)
        lower = (product - upper.astype(F32)).astype(BF16)
        part = lax.dot_general(upper, member, CONTRACT_LAST, preferred_element_type=F32)
        part += lax.dot_general(lower, member, CONTRACT_LAST, preferred_element_type=F32)
        narrow.append(part.astype(BF16))
    left = jnp.concatenate(narrow, axis=1)
    blocks = []
    for i in range(mine):
        right = jnp.concatenate(
            [w[i * group_examples : (i + 1) * group_examples, :] for w in wide], axis=0
        )
        blocks.append(jnp.dot(left, right, preferred_element_type=F32))
    out[...] = jnp.concatenate(blocks, axis=1) * scale


def by_tokens(hidden_in, out_grads, piece_of, owner_dp, owner_slot, sketch_in, sketch_out):
    count_dp = lax.axis_size("dp")
    count_fsdp = lax.axis_size("fsdp")
    token_rows = hidden_in.shape[0]
    width = sketch_in.shape[1]
    owned = count_dp // 2
    bits = bits_of(count_fsdp)
    low, top = bits[:-1], bits[-1]
    own_out, own_in = sketch_out.T, sketch_in.T
    near_out = spread(own_out, low)
    far_out = swap(own_out, "fsdp", top)
    near_in = spread(own_in, low)
    near = list(range(top))
    inputs = project(near_in, near, hidden_in, None, F32)
    far_in = swap(own_in, "fsdp", top)
    out_shards = near_out + spread(after(far_out, inputs), low)
    errors = pl.pallas_call(
        functools.partial(errors_kernel, list(range(count_fsdp)), owned),
        out_shape=jax.ShapeDtypeStruct((width + KEY_ROWS, token_rows), BF16),
        in_specs=[VMEM] * (count_fsdp + 2) + [SMEM] * 2 + [ANY],
        out_specs=VMEM,
        compiler_params=ROOM,
        cost_estimate=pl.CostEstimate(flops=30_000_000_000, bytes_accessed=60_000_000, transcendentals=0),
    )(*out_shards, out_grads, piece_of, owner_dp, owner_slot, inputs)
    group_errors, halfway = gather_group(errors)
    far_in = spread(after(far_in, halfway), low)
    for k, shard in enumerate(far_in):
        last = k == len(far_in) - 1
        inputs = project([shard], [top + k], hidden_in, inputs, BF16 if last else F32)
    group_inputs, _ = gather_group(inputs)
    all_errors = spread(group_errors, bits)
    all_inputs = spread(group_inputs, bits)
    scale = 1.0 / math.sqrt(owned * count_dp * count_fsdp)
    return pl.pallas_call(
        functools.partial(gram_kernel, count_dp, owned * count_dp, scale),
        out_shape=jax.ShapeDtypeStruct((GR // count_dp, width * width // count_fsdp), F32),
        in_specs=[VMEM] * (2 * count_fsdp),
        out_specs=VMEM,
        compiler_params=ROOM,
    )(*all_errors, *all_inputs)


def by_pieces(hidden_in, out_grads, piece_of, owner_dp, owner_slot, sketch_in, sketch_out):
    count_dp = lax.axis_size("dp")
    count_fsdp = lax.axis_size("fsdp")
    full_in, full_out = (
        lax.all_gather(sketch_in, "fsdp", axis=0, tiled=True),
        lax.all_gather(sketch_out, "fsdp", axis=0, tiled=True),
    )
    inputs_low = jnp.dot(hidden_in, full_in, preferred_element_type=F32).astype(BF16)
    errors_low = jnp.dot(out_grads, full_out, preferred_element_type=F32).astype(BF16)
    rows_here = inputs_low.shape[0]
    width = inputs_low.shape[1]
    pieces = owner_dp.shape[1]
    member = piece_of[0][:, None] == jnp.arange(pieces, dtype=jnp.int32)[None, :]
    spread = (member.astype(BF16)[:, :, None] * inputs_low[:, None, :]).reshape(
        rows_here, pieces * width
    )
    partial_value = lax.dot_general(
        spread, errors_low, (((0,), (0,)), ((), ())), preferred_element_type=F32
    )
    partial_value = partial_value.reshape(pieces, width * width)
    target = owner_dp[0]
    earlier = jnp.arange(pieces)[None, :] < jnp.arange(pieces)[:, None]
    ranked = jnp.sum(((target[:, None] == target[None, :]) & earlier).astype(jnp.int32), axis=1)
    places = target * CAP + ranked
    slots_total = count_dp * CAP
    routing_mask = places[None, :] == jnp.arange(slots_total, dtype=jnp.int32)[:, None]
    outgoing = jnp.dot(routing_mask.astype(F32), partial_value, precision=lax.Precision.HIGHEST)
    labels = jnp.sum(routing_mask.astype(jnp.int32) * (owner_slot[0][None, :] + 1), axis=1) - 1
    incoming, arrived = (
        lax.all_to_all(outgoing, "dp", split_axis=0, concat_axis=0, tiled=True),
        lax.all_to_all(labels, "dp", split_axis=0, concat_axis=0, tiled=True),
    )
    owned = count_dp // 2
    collect = (arrived[None, :] == jnp.arange(owned, dtype=jnp.int32)[:, None]).astype(F32)
    features = jnp.dot(collect, incoming, precision=lax.Precision.HIGHEST).astype(BF16)
    local_gram = lax.dot_general(
        features[:, :GR], features, (((0,), (0,)), ((), ())), preferred_element_type=F32
    )
    scale_factor = 1.0 / math.sqrt(owned * count_dp * count_fsdp)
    section_one = lax.psum_scatter(local_gram, "fsdp", scatter_dimension=1, tiled=True)
    result = lax.psum_scatter(section_one, "dp", scatter_dimension=0, tiled=True)
    return result * scale_factor


def on_device(hidden_in, out_grads, piece_of, owner_dp, owner_slot, sketch_in, sketch_out):
    count_dp = lax.axis_size("dp")
    count_fsdp = lax.axis_size("fsdp")
    token_rows = hidden_in.shape[0]
    width = sketch_in.shape[1]
    gathered = count_dp * count_fsdp * token_rows * 2 * width * 2
    summed = GR * width * width * 4
    doubling = all(n & (n - 1) == 0 for n in (count_dp, count_fsdp))
    whole_tiles = token_rows % 128 == 0 and width % (16 * count_fsdp) == 0
    exact_keys = count_dp * (count_dp // 2) <= 256
    form = by_tokens if gathered <= summed and doubling and whole_tiles and exact_keys else by_pieces
    return form(hidden_in, out_grads, piece_of, owner_dp, owner_slot, sketch_in, sketch_out)


def solution(mesh):
    return jax.shard_map(
        on_device,
        mesh=mesh,
        in_specs=(
            P(("dp", "fsdp"), None),
            P(("dp", "fsdp"), None),
            P(("dp", "fsdp"), None),
            P(("dp", "fsdp"), None),
            P(("dp", "fsdp"), None),
            P("fsdp", None),
            P("fsdp", None),
        ),
        out_specs=P("dp", "fsdp"),
        check_vma=False,
    )
```

```python
import functools
import math

import jax
import jax.numpy as jnp
from jax import lax
from jax.experimental import pallas as pl
from jax.experimental.pallas import tpu as pltpu
from jax.sharding import PartitionSpec as P

CAP = 2
GR = 192
BF16 = jnp.bfloat16
F32 = jnp.float32
BOTH = ("dp", "fsdp")
CONTRACT_LAST = (((1,), (1,)), ((), ()))
VMEM = pl.BlockSpec(memory_space=pltpu.VMEM)
SMEM = pl.BlockSpec(memory_space=pltpu.SMEM)
ANY = pl.BlockSpec(memory_space=pl.ANY)
ERRORS_COST = pl.CostEstimate(
    flops=1_500_000_000, bytes_accessed=1_000_000, transcendentals=0
)
PICKED_COST = pl.CostEstimate(
    flops=2_000_000_000, bytes_accessed=1_000_000, transcendentals=0
)
ROOM = pltpu.CompilerParams(vmem_limit_bytes=16 * 1024 * 1024)


def swap(value, axis, bit):
    count = lax.axis_size(axis)
    return lax.ppermute(value, axis, [(i, i ^ bit) for i in range(count)])


def bits_of(count):
    return [1 << k for k in range(count.bit_length() - 1)]


def after(value, *others):
    return lax.optimization_barrier((value, *others))[0]


def widen(rows, axis, bit):
    return jnp.concatenate([rows, swap(rows, axis, bit)], axis=0)


def spread(value, bits):
    held = {0: value}
    for bit in reversed(bits):
        held.update({k ^ bit: swap(v, "fsdp", bit) for k, v in list(held.items())})
    return [held[k] for k in range(len(held))]


def low_rank(sketches, which, tokens):
    me = lax.axis_index("fsdp")
    total = 0.0
    for sketch, k in zip(sketches, which):
        size = sketch.shape[1]
        start = pl.multiple_of((me ^ k) * size, size)
        total += lax.dot_general(
            sketch[...], tokens[:, pl.ds(start, size)], CONTRACT_LAST, preferred_element_type=F32
        )
    return total


def near_kernel(which, *refs):
    refs[-1][...] = low_rank(refs[: len(which)], which, refs[-2])


def project_kernel(which, *refs):
    count = len(which)
    tokens, total, out = refs[count:]
    out[...] = low_rank(refs[:count], which, tokens) + total[...]


def keys_kernel(owned, piece_of, owner_dp, owner_slot, _, out):
    piece = piece_of[...]
    key = jnp.zeros(piece.shape, jnp.int32)
    for p in range(owner_dp.shape[1]):
        key = jnp.where(piece == p, owner_dp[0, p] * owned + owner_slot[0, p], key)
    out[...] = jnp.broadcast_to(key.astype(F32), out.shape).astype(BF16)


def message_kernel(which, mine, lead, *refs):
    count = len(which)
    tokens, total, keys, out = refs[count:]
    rows = (low_rank(refs[:count], which, tokens) + total[...]).astype(BF16)
    shared = jnp.concatenate([rows[:lead, :], keys[lead:, :]], axis=0)
    parts = rows.shape[0] // mine
    for k in range(out.shape[0]):
        f = k % parts
        out[k, :mine, :] = rows[f * mine : (f + 1) * mine, :]
        out[k, mine:, :] = shared


def call(kernel, operands, outputs, specs=None, cost=None):
    return pl.pallas_call(
        kernel,
        out_shape=outputs,
        in_specs=specs or [VMEM] * len(operands),
        out_specs=VMEM,
        compiler_params=ROOM,
        cost_estimate=cost,
    )(*operands)


def errors_kernel(which, *refs):
    count = len(which)
    refs[-1][...] = low_rank(refs[:count], which, refs[count]).astype(BF16)


def picked_kernel(*refs):
    out = refs[-1]
    rows, count = out.shape[0], out.shape[1] // refs[0].shape[1]
    width = len(refs[:-1]) * refs[0].shape[0] // count
    column = lax.axis_index("dp") * rows + lax.broadcasted_iota(jnp.int32, (rows, width), 0)
    at = lax.broadcasted_iota(jnp.int32, (rows, width), 1)
    pick = (at == column % width).astype(F32).astype(BF16)
    err = jnp.concatenate(
        [ref[k : k + width, :] for ref in refs[:-1] for k in range(0, ref.shape[0], width)], axis=1
    )
    out[...] = jnp.dot(pick, err, preferred_element_type=F32)


def gram_kernel(order, lead, group_examples, scale, *refs):
    errors, picked, messages, out = refs[:-3], refs[-3], refs[-2], refs[-1]
    count_fsdp, count_dp = len(errors), len(order)
    rows_here, columns_here = out.shape
    width = errors[0].shape[0] // count_dp
    mine = columns_here // width
    size = messages.shape[1]
    d, f = lax.axis_index("dp"), lax.axis_index("fsdp")
    place = (rows_here, size - mine)
    column = d * rows_here + lax.broadcasted_iota(jnp.int32, place, 0)
    pick_in = (lax.broadcasted_iota(jnp.int32, place, 1) == column // width).astype(F32).astype(BF16)
    wide, narrow = [], []
    for g, e_ref in enumerate(errors):
        places = [(d ^ k) * count_fsdp + (f ^ g) for k in order]
        err = jnp.concatenate([e_ref[k * width : (k + 1) * width, :] for k in range(count_dp)], axis=1)
        here = jnp.concatenate([messages[k, :mine, :] for k in places], axis=1)
        shared = jnp.concatenate([messages[k, mine:, :] for k in places], axis=1)
        key = shared.astype(F32)[lead : lead + 1, :]
        tokens = key.shape[1]
        example = lax.broadcasted_iota(jnp.int32, (group_examples, tokens), 0).astype(F32)
        member = (example == key).astype(F32).astype(BF16)
        spread_rows = jnp.concatenate([member * here[i : i + 1, :] for i in range(mine)], axis=0)
        wide.append(
            lax.dot_general(spread_rows, err, CONTRACT_LAST, preferred_element_type=F32).astype(BF16)
        )
        product = jnp.dot(pick_in, shared, preferred_element_type=F32)
        product = product * picked[:, g * tokens : (g + 1) * tokens]
        upper = product.astype(BF16)
        lower = (product - upper.astype(F32)).astype(BF16)
        part = lax.dot_general(upper, member, CONTRACT_LAST, preferred_element_type=F32)
        part += lax.dot_general(lower, member, CONTRACT_LAST, preferred_element_type=F32)
        narrow.append(part.astype(BF16))
    left = jnp.concatenate(narrow, axis=1)
    blocks = []
    for i in range(mine):
        right = jnp.concatenate(
            [w[i * group_examples : (i + 1) * group_examples, :] for w in wide], axis=0
        )
        blocks.append(jnp.dot(left, right, preferred_element_type=F32))
    out[...] = jnp.concatenate(blocks, axis=1) * scale


def by_tokens(hidden_in, out_grads, piece_of, owner_dp, owner_slot, sketch_in, sketch_out):
    count_dp = lax.axis_size("dp")
    count_fsdp = lax.axis_size("fsdp")
    token_rows = hidden_in.shape[0]
    width = sketch_in.shape[1]
    owned = count_dp // 2
    bits = bits_of(count_fsdp)
    low, top = bits[:-1], bits[-1]
    mine = width // count_fsdp
    lead = -(-GR // width)
    tile = (lead + 16) // 16 * 16
    rows_here = GR // count_dp
    square = jax.ShapeDtypeStruct((width, token_rows), F32)
    own_out, own_in = sketch_out.T, sketch_in.T

    near_out = spread(own_out, low)
    far_out = swap(own_out, "fsdp", top)
    near_in = spread(own_in, low)
    far_in = swap(own_in, "fsdp", top)
    inputs = call(functools.partial(near_kernel, list(range(top))), [*near_in, hidden_in], square)
    out_shards = near_out + spread(after(far_out, inputs), low)
    errors = call(
        functools.partial(errors_kernel, list(range(count_fsdp))),
        [*out_shards, out_grads, inputs],
        jax.ShapeDtypeStruct(square.shape, BF16),
        [VMEM] * (count_fsdp + 1) + [ANY],
        ERRORS_COST,
    )
    first, *later = bits_of(count_dp)
    order = [0]
    for bit in [*later, first]:
        order += [k ^ bit for k in order]
    keys = None
    for bit in later:
        errors = widen(errors, "dp", bit)
        far_in = after(far_in, errors)
        if keys is None:
            keys = call(
                functools.partial(keys_kernel, owned),
                [piece_of, owner_dp, owner_slot, errors],
                jax.ShapeDtypeStruct((tile, token_rows), BF16),
                [VMEM, SMEM, SMEM, ANY],
            )
    far_in = spread(far_in, low)
    for k in range(top - 1):
        inputs = call(
            functools.partial(project_kernel, [top + k]), [far_in[k], hidden_in, inputs], square
        )
    messages = call(
        functools.partial(message_kernel, [2 * top - 1], mine, lead),
        [far_in[-1], hidden_in, inputs, keys],
        jax.ShapeDtypeStruct((count_dp * count_fsdp, mine + tile, token_rows), BF16),
    )
    messages = lax.all_to_all(messages, BOTH, split_axis=0, concat_axis=0, tiled=True)
    all_errors = spread(widen(errors, "dp", first), bits)
    picked = call(
        picked_kernel,
        all_errors,
        jax.ShapeDtypeStruct((rows_here, count_dp * count_fsdp * token_rows), F32),
        cost=PICKED_COST,
    )
    scale = 1.0 / math.sqrt(owned * count_dp * count_fsdp)
    return call(
        functools.partial(gram_kernel, order, lead, owned * count_dp, scale),
        [*all_errors, picked, messages],
        jax.ShapeDtypeStruct((rows_here, width * width // count_fsdp), F32),
    )


def by_pieces(hidden_in, out_grads, piece_of, owner_dp, owner_slot, sketch_in, sketch_out):
    count_dp = lax.axis_size("dp")
    count_fsdp = lax.axis_size("fsdp")
    full_in, full_out = (
        lax.all_gather(sketch_in, "fsdp", axis=0, tiled=True),
        lax.all_gather(sketch_out, "fsdp", axis=0, tiled=True),
    )
    inputs_low = jnp.dot(hidden_in, full_in, preferred_element_type=F32).astype(BF16)
    errors_low = jnp.dot(out_grads, full_out, preferred_element_type=F32).astype(BF16)
    rows_here = inputs_low.shape[0]
    width = inputs_low.shape[1]
    pieces = owner_dp.shape[1]
    member = piece_of[0][:, None] == jnp.arange(pieces, dtype=jnp.int32)[None, :]
    spread = (member.astype(BF16)[:, :, None] * inputs_low[:, None, :]).reshape(
        rows_here, pieces * width
    )
    partial_value = lax.dot_general(
        spread, errors_low, (((0,), (0,)), ((), ())), preferred_element_type=F32
    )
    partial_value = partial_value.reshape(pieces, width * width)
    target = owner_dp[0]
    earlier = jnp.arange(pieces)[None, :] < jnp.arange(pieces)[:, None]
    ranked = jnp.sum(((target[:, None] == target[None, :]) & earlier).astype(jnp.int32), axis=1)
    places = target * CAP + ranked
    slots_total = count_dp * CAP
    routing_mask = places[None, :] == jnp.arange(slots_total, dtype=jnp.int32)[:, None]
    outgoing = jnp.dot(routing_mask.astype(F32), partial_value, precision=lax.Precision.HIGHEST)
    labels = jnp.sum(routing_mask.astype(jnp.int32) * (owner_slot[0][None, :] + 1), axis=1) - 1
    incoming, arrived = (
        lax.all_to_all(outgoing, "dp", split_axis=0, concat_axis=0, tiled=True),
        lax.all_to_all(labels, "dp", split_axis=0, concat_axis=0, tiled=True),
    )
    owned = count_dp // 2
    collect = (arrived[None, :] == jnp.arange(owned, dtype=jnp.int32)[:, None]).astype(F32)
    features = jnp.dot(collect, incoming, precision=lax.Precision.HIGHEST).astype(BF16)
    local_gram = lax.dot_general(
        features[:, :GR], features, (((0,), (0,)), ((), ())), preferred_element_type=F32
    )
    scale_factor = 1.0 / math.sqrt(owned * count_dp * count_fsdp)
    section_one = lax.psum_scatter(local_gram, "fsdp", scatter_dimension=1, tiled=True)
    result = lax.psum_scatter(section_one, "dp", scatter_dimension=0, tiled=True)
    return result * scale_factor


def on_device(hidden_in, out_grads, piece_of, owner_dp, owner_slot, sketch_in, sketch_out):
    count_dp = lax.axis_size("dp")
    count_fsdp = lax.axis_size("fsdp")
    token_rows = hidden_in.shape[0]
    width = sketch_in.shape[1]
    gathered = count_dp * count_fsdp * token_rows * 2 * width * 2
    summed = GR * width * width * 4
    doubling = all(n > 1 and n & (n - 1) == 0 for n in (count_dp, count_fsdp))
    whole_tiles = token_rows % 128 == 0 and width % (16 * count_fsdp) == 0
    exact_keys = count_dp * (count_dp // 2) <= 256
    form = by_tokens if gathered <= summed and doubling and whole_tiles and exact_keys else by_pieces
    return form(hidden_in, out_grads, piece_of, owner_dp, owner_slot, sketch_in, sketch_out)


def solution(mesh):
    return jax.shard_map(
        on_device,
        mesh=mesh,
        in_specs=(
            P(("dp", "fsdp"), None),
            P(("dp", "fsdp"), None),
            P(("dp", "fsdp"), None),
            P(("dp", "fsdp"), None),
            P(("dp", "fsdp"), None),
            P("fsdp", None),
            P("fsdp", None),
        ),
        out_specs=P("dp", "fsdp"),
        check_vma=False,
    )
```

```python
import functools
import math

import jax
import jax.numpy as jnp
from jax import lax
from jax.experimental import pallas as pl
from jax.experimental.pallas import tpu as pltpu
from jax.sharding import PartitionSpec as P

CAP = 2
GR = 192
BF16 = jnp.bfloat16
F32 = jnp.float32
BOTH = ("dp", "fsdp")
CONTRACT_LAST = (((1,), (1,)), ((), ()))
VMEM = pl.BlockSpec(memory_space=pltpu.VMEM)
SMEM = pl.BlockSpec(memory_space=pltpu.SMEM)
ANY = pl.BlockSpec(memory_space=pl.ANY)
ERRORS_COST = pl.CostEstimate(
    flops=1_500_000_000, bytes_accessed=1_000_000, transcendentals=0
)
PICKED_COST = pl.CostEstimate(
    flops=600_000_000, bytes_accessed=1_000_000, transcendentals=0
)
ROOM = pltpu.CompilerParams(vmem_limit_bytes=16 * 1024 * 1024)


def swap(value, axis, bit):
    count = lax.axis_size(axis)
    return lax.ppermute(value, axis, [(i, i ^ bit) for i in range(count)])


def bits_of(count):
    return [1 << k for k in range(count.bit_length() - 1)]


def after(value, *others):
    return lax.optimization_barrier((value, *others))[0]


def widen(rows, axis, bit):
    return jnp.concatenate([rows, swap(rows, axis, bit)], axis=0)


def spread(value, bits):
    held = {0: value}
    for bit in reversed(bits):
        held.update({k ^ bit: swap(v, "fsdp", bit) for k, v in list(held.items())})
    return [held[k] for k in range(len(held))]


def low_rank(sketches, which, tokens):
    me = lax.axis_index("fsdp")
    total = 0.0
    for sketch, k in zip(sketches, which):
        size = sketch.shape[1]
        start = pl.multiple_of((me ^ k) * size, size)
        total += lax.dot_general(
            sketch[...], tokens[:, pl.ds(start, size)], CONTRACT_LAST, preferred_element_type=F32
        )
    return total


def near_kernel(which, *refs):
    refs[-1][...] = low_rank(refs[: len(which)], which, refs[-2])


def project_kernel(which, *refs):
    count = len(which)
    tokens, total, out = refs[count:]
    out[...] = low_rank(refs[:count], which, tokens) + total[...]


def keys_kernel(owned, piece_of, owner_dp, owner_slot, _, out):
    piece = piece_of[...]
    key = jnp.zeros(piece.shape, jnp.int32)
    for p in range(owner_dp.shape[1]):
        key = jnp.where(piece == p, owner_dp[0, p] * owned + owner_slot[0, p], key)
    out[...] = jnp.broadcast_to(key.astype(F32), out.shape).astype(BF16)


def message_kernel(which, mine, lead, *refs):
    count = len(which)
    tokens, total, keys, out = refs[count:]
    rows = (low_rank(refs[:count], which, tokens) + total[...]).astype(BF16)
    shared = jnp.concatenate([rows[:lead, :], keys[: out.shape[1] - mine - lead, :]], axis=0)
    parts = rows.shape[0] // mine
    for k in range(out.shape[0]):
        f = k % parts
        out[k] = jnp.concatenate([rows[f * mine : (f + 1) * mine, :], shared], axis=0)


def call(kernel, operands, outputs, specs=None, cost=None):
    return pl.pallas_call(
        kernel,
        out_shape=outputs,
        in_specs=specs or [VMEM] * len(operands),
        out_specs=VMEM,
        compiler_params=ROOM,
        cost_estimate=cost,
    )(*operands)


def errors_kernel(which, *refs):
    count = len(which)
    refs[-1][...] = low_rank(refs[:count], which, refs[count]).astype(BF16)


def picked_kernel(*refs):
    out = refs[-1]
    rows, count = out.shape[0], out.shape[1] // refs[0].shape[1]
    width = len(refs[:-1]) * refs[0].shape[0] // count
    column = lax.axis_index("dp") * rows + lax.broadcasted_iota(jnp.int32, (rows, width), 0)
    at = lax.broadcasted_iota(jnp.int32, (rows, width), 1)
    pick = (at == column % width).astype(F32).astype(BF16)
    err = jnp.concatenate(
        [ref[k : k + width, :] for ref in refs[:-1] for k in range(0, ref.shape[0], width)], axis=1
    )
    out[...] = jnp.dot(pick, err, preferred_element_type=F32)


def gram_kernel(order, lead, group_examples, scale, *refs):
    errors, picked, messages, out = refs[:-3], refs[-3], refs[-2], refs[-1]
    count_fsdp, count_dp = len(errors), len(order)
    rows_here, columns_here = out.shape
    width = errors[0].shape[0] // count_dp
    mine = columns_here // width
    d, f = lax.axis_index("dp"), lax.axis_index("fsdp")
    wide, narrow = [], []
    for g, e_ref in enumerate(errors):
        places = [(d ^ k) * count_fsdp + (f ^ g) for k in order]
        err = jnp.concatenate([e_ref[k * width : (k + 1) * width, :] for k in range(count_dp)], axis=1)
        held = jnp.concatenate([messages[k] for k in places], axis=1)
        here, shared = held[:mine, :], held[mine:, :]
        key = shared.astype(F32)[lead : lead + 1, :]
        tokens = key.shape[1]
        example = lax.broadcasted_iota(jnp.int32, (group_examples, tokens), 0).astype(F32)
        member = (example == key).astype(F32).astype(BF16)
        spread_rows = [member * here[i : i + 1, :] for i in range(mine)]
        spread_rows = jnp.concatenate(
            [jnp.concatenate(spread_rows[i : i + 2], axis=1) for i in range(0, mine, 2)], axis=0
        )
        blank = jnp.zeros_like(err)
        twice = jnp.concatenate(
            [jnp.concatenate([err, blank], axis=1), jnp.concatenate([blank, err], axis=1)], axis=0
        )
        wide.append(
            lax.dot_general(spread_rows, twice, CONTRACT_LAST, preferred_element_type=F32).astype(BF16)
        )
        column = d * rows_here + lax.broadcasted_iota(jnp.int32, (rows_here, tokens), 0)
        shared = shared.astype(F32)
        chosen = shared[:1, :]
        for i in range(1, lead):
            chosen = jnp.where(column >= i * width, shared[i : i + 1, :], chosen)
        product = chosen * picked[:, g * tokens : (g + 1) * tokens]
        upper = product.astype(BF16)
        lower = (product - upper.astype(F32)).astype(BF16)
        part = lax.dot_general(upper, member, CONTRACT_LAST, preferred_element_type=F32)
        part += lax.dot_general(lower, member, CONTRACT_LAST, preferred_element_type=F32)
        narrow.append(part.astype(BF16))
    left = jnp.concatenate(narrow, axis=1)
    blocks = []
    for i in range(mine // 2):
        right = jnp.concatenate(
            [w[i * group_examples : (i + 1) * group_examples, :] for w in wide], axis=0
        )
        blocks.append(jnp.dot(left, right, preferred_element_type=F32))
    out[...] = jnp.concatenate(blocks, axis=1) * scale


def by_tokens(hidden_in, out_grads, piece_of, owner_dp, owner_slot, sketch_in, sketch_out):
    count_dp = lax.axis_size("dp")
    count_fsdp = lax.axis_size("fsdp")
    token_rows = hidden_in.shape[0]
    width = sketch_in.shape[1]
    owned = count_dp // 2
    bits = bits_of(count_fsdp)
    low, top = bits[:-1], bits[-1]
    mine = width // count_fsdp
    lead = -(-GR // width)
    tile = (lead + 8) // 8 * 8
    rows_here = GR // count_dp
    square = jax.ShapeDtypeStruct((width, token_rows), F32)
    own_out, own_in = sketch_out.T, sketch_in.T

    near_out = spread(own_out, low)
    far_out = swap(own_out, "fsdp", top)
    near_in = spread(own_in, low)
    far_in = swap(own_in, "fsdp", top)
    inputs = call(functools.partial(near_kernel, list(range(top))), [*near_in, hidden_in], square)
    out_shards = near_out + spread(after(far_out, inputs), low)
    keys = call(
        functools.partial(keys_kernel, owned),
        [piece_of, owner_dp, owner_slot, inputs],
        jax.ShapeDtypeStruct((16, token_rows), BF16),
        [VMEM, SMEM, SMEM, ANY],
    )
    errors = call(
        functools.partial(errors_kernel, list(range(count_fsdp))),
        [*out_shards, out_grads, inputs, keys],
        jax.ShapeDtypeStruct(square.shape, BF16),
        [VMEM] * (count_fsdp + 1) + [ANY] * 2,
        ERRORS_COST,
    )
    first, *later = bits_of(count_dp)
    order = [0]
    for bit in [*later, first]:
        order += [k ^ bit for k in order]
    for bit in later:
        errors = widen(errors, "dp", bit)
        far_in = after(far_in, errors)
    far_in = spread(far_in, low)
    for k in range(top - 1):
        inputs = call(
            functools.partial(project_kernel, [top + k]), [far_in[k], hidden_in, inputs], square
        )
    messages = call(
        functools.partial(message_kernel, [2 * top - 1], mine, lead),
        [far_in[-1], hidden_in, inputs, keys],
        jax.ShapeDtypeStruct((count_dp * count_fsdp, mine + tile, token_rows), BF16),
    )
    messages = lax.all_to_all(messages, BOTH, split_axis=0, concat_axis=0, tiled=True)
    all_errors = spread(widen(errors, "dp", first), bits)
    picked = call(
        picked_kernel,
        all_errors,
        jax.ShapeDtypeStruct((rows_here, count_dp * count_fsdp * token_rows), F32),
        cost=PICKED_COST,
    )
    scale = 1.0 / math.sqrt(owned * count_dp * count_fsdp)
    return call(
        functools.partial(gram_kernel, order, lead, owned * count_dp, scale),
        [*all_errors, picked, messages],
        jax.ShapeDtypeStruct((rows_here, width * width // count_fsdp), F32),
    )


def by_pieces(hidden_in, out_grads, piece_of, owner_dp, owner_slot, sketch_in, sketch_out):
    count_dp = lax.axis_size("dp")
    count_fsdp = lax.axis_size("fsdp")
    full_in, full_out = (
        lax.all_gather(sketch_in, "fsdp", axis=0, tiled=True),
        lax.all_gather(sketch_out, "fsdp", axis=0, tiled=True),
    )
    inputs_low = jnp.dot(hidden_in, full_in, preferred_element_type=F32).astype(BF16)
    errors_low = jnp.dot(out_grads, full_out, preferred_element_type=F32).astype(BF16)
    rows_here = inputs_low.shape[0]
    width = inputs_low.shape[1]
    pieces = owner_dp.shape[1]
    member = piece_of[0][:, None] == jnp.arange(pieces, dtype=jnp.int32)[None, :]
    spread = (member.astype(BF16)[:, :, None] * inputs_low[:, None, :]).reshape(
        rows_here, pieces * width
    )
    partial_value = lax.dot_general(
        spread, errors_low, (((0,), (0,)), ((), ())), preferred_element_type=F32
    )
    partial_value = partial_value.reshape(pieces, width * width)
    target = owner_dp[0]
    earlier = jnp.arange(pieces)[None, :] < jnp.arange(pieces)[:, None]
    ranked = jnp.sum(((target[:, None] == target[None, :]) & earlier).astype(jnp.int32), axis=1)
    places = target * CAP + ranked
    slots_total = count_dp * CAP
    routing_mask = places[None, :] == jnp.arange(slots_total, dtype=jnp.int32)[:, None]
    outgoing = jnp.dot(routing_mask.astype(F32), partial_value, precision=lax.Precision.HIGHEST)
    labels = jnp.sum(routing_mask.astype(jnp.int32) * (owner_slot[0][None, :] + 1), axis=1) - 1
    incoming, arrived = (
        lax.all_to_all(outgoing, "dp", split_axis=0, concat_axis=0, tiled=True),
        lax.all_to_all(labels, "dp", split_axis=0, concat_axis=0, tiled=True),
    )
    owned = count_dp // 2
    collect = (arrived[None, :] == jnp.arange(owned, dtype=jnp.int32)[:, None]).astype(F32)
    features = jnp.dot(collect, incoming, precision=lax.Precision.HIGHEST).astype(BF16)
    local_gram = lax.dot_general(
        features[:, :GR], features, (((0,), (0,)), ((), ())), preferred_element_type=F32
    )
    scale_factor = 1.0 / math.sqrt(owned * count_dp * count_fsdp)
    section_one = lax.psum_scatter(local_gram, "fsdp", scatter_dimension=1, tiled=True)
    result = lax.psum_scatter(section_one, "dp", scatter_dimension=0, tiled=True)
    return result * scale_factor


def on_device(hidden_in, out_grads, piece_of, owner_dp, owner_slot, sketch_in, sketch_out):
    count_dp = lax.axis_size("dp")
    count_fsdp = lax.axis_size("fsdp")
    token_rows = hidden_in.shape[0]
    width = sketch_in.shape[1]
    gathered = count_dp * count_fsdp * token_rows * 2 * width * 2
    summed = GR * width * width * 4
    doubling = all(n > 1 and n & (n - 1) == 0 for n in (count_dp, count_fsdp))
    whole_tiles = token_rows % 128 == 0 and width % (16 * count_fsdp) == 0
    exact_keys = count_dp * (count_dp // 2) <= 256
    form = by_tokens if gathered <= summed and doubling and whole_tiles and exact_keys else by_pieces
    return form(hidden_in, out_grads, piece_of, owner_dp, owner_slot, sketch_in, sketch_out)


def solution(mesh):
    return jax.shard_map(
        on_device,
        mesh=mesh,
        in_specs=(
            P(("dp", "fsdp"), None),
            P(("dp", "fsdp"), None),
            P(("dp", "fsdp"), None),
            P(("dp", "fsdp"), None),
            P(("dp", "fsdp"), None),
            P("fsdp", None),
            P("fsdp", None),
        ),
        out_specs=P("dp", "fsdp"),
        check_vma=False,
    )
```

```python
import functools
import math

import jax
import jax.numpy as jnp
from jax import lax
from jax.experimental import pallas as pl
from jax.experimental.pallas import tpu as pltpu
from jax.sharding import PartitionSpec as P

CAP = 2
GR = 192
BF16 = jnp.bfloat16
F32 = jnp.float32
BOTH = ("dp", "fsdp")
CONTRACT_LAST = (((1,), (1,)), ((), ()))
VMEM = pl.BlockSpec(memory_space=pltpu.VMEM)
SMEM = pl.BlockSpec(memory_space=pltpu.SMEM)
ANY = pl.BlockSpec(memory_space=pl.ANY)
ERRORS_COST = pl.CostEstimate(
    flops=1_500_000_000, bytes_accessed=1_000_000, transcendentals=0
)
PICKED_COST = pl.CostEstimate(
    flops=600_000_000, bytes_accessed=1_000_000, transcendentals=0
)
ROOM = pltpu.CompilerParams(vmem_limit_bytes=16 * 1024 * 1024)


def swap(value, axis, bit):
    count = lax.axis_size(axis)
    return lax.ppermute(value, axis, [(i, i ^ bit) for i in range(count)])


def bits_of(count):
    return [1 << k for k in range(count.bit_length() - 1)]


def after(value, *others):
    return lax.optimization_barrier((value, *others))[0]


def widen(rows, axis, bit):
    return jnp.concatenate([rows, swap(rows, axis, bit)], axis=0)


def spread(value, bits):
    held = {0: value}
    for bit in reversed(bits):
        held.update({k ^ bit: swap(v, "fsdp", bit) for k, v in list(held.items())})
    return [held[k] for k in range(len(held))]


def low_rank(sketches, which, tokens):
    me = lax.axis_index("fsdp")
    total = 0.0
    for sketch, k in zip(sketches, which):
        size = sketch.shape[1]
        start = pl.multiple_of((me ^ k) * size, size)
        total += lax.dot_general(
            sketch[...], tokens[:, pl.ds(start, size)], CONTRACT_LAST, preferred_element_type=F32
        )
    return total


def near_kernel(which, *refs):
    refs[-1][...] = low_rank(refs[: len(which)], which, refs[-2])


def project_kernel(which, *refs):
    count = len(which)
    tokens, total, out = refs[count:]
    out[...] = low_rank(refs[:count], which, tokens) + total[...]


def keys_kernel(owned, piece_of, owner_dp, owner_slot, _, out):
    piece = piece_of[...]
    key = jnp.zeros(piece.shape, jnp.int32)
    for p in range(owner_dp.shape[1]):
        key = jnp.where(piece == p, owner_dp[0, p] * owned + owner_slot[0, p], key)
    out[...] = jnp.broadcast_to(key.astype(F32), out.shape).astype(BF16)


def message_kernel(which, mine, lead, *refs):
    count = len(which)
    tokens, total, keys, out = refs[count:]
    rows = (low_rank(refs[:count], which, tokens) + total[...]).astype(BF16)
    shared = jnp.concatenate([rows[:lead, :], keys[: out.shape[1] - mine - lead, :]], axis=0)
    parts = rows.shape[0] // mine
    for k in range(out.shape[0]):
        f = k % parts
        out[k] = jnp.concatenate([rows[f * mine : (f + 1) * mine, :], shared], axis=0)


def call(kernel, operands, outputs, specs=None, cost=None):
    return pl.pallas_call(
        kernel,
        out_shape=outputs,
        in_specs=specs or [VMEM] * len(operands),
        out_specs=VMEM,
        compiler_params=ROOM,
        cost_estimate=cost,
    )(*operands)


def errors_kernel(which, *refs):
    count = len(which)
    refs[-1][...] = low_rank(refs[:count], which, refs[count]).astype(BF16)


def picked_kernel(*refs):
    out = refs[-1]
    rows, count = out.shape[0], out.shape[1] // refs[0].shape[1]
    width = len(refs[:-1]) * refs[0].shape[0] // count
    column = lax.axis_index("dp") * rows + lax.broadcasted_iota(jnp.int32, (rows, width), 0)
    at = lax.broadcasted_iota(jnp.int32, (rows, width), 1)
    pick = (at == column % width).astype(F32).astype(BF16)
    err = jnp.concatenate(
        [ref[k : k + width, :] for ref in refs[:-1] for k in range(0, ref.shape[0], width)], axis=1
    )
    out[...] = jnp.dot(pick, err, preferred_element_type=F32)


def gram_kernel(order, lead, group_examples, scale, *refs):
    errors, picked, messages, out = refs[:-3], refs[-3], refs[-2], refs[-1]
    count_fsdp, count_dp = len(errors), len(order)
    rows_here, columns_here = out.shape
    width = errors[0].shape[0] // count_dp
    mine = columns_here // width
    d, f = lax.axis_index("dp"), lax.axis_index("fsdp")
    wide, narrow = [], []
    for g, e_ref in enumerate(errors):
        places = [(d ^ k) * count_fsdp + (f ^ g) for k in order]
        err = jnp.concatenate([e_ref[k * width : (k + 1) * width, :] for k in range(count_dp)], axis=1)
        held = jnp.concatenate([messages[k] for k in places], axis=1)
        here, shared = held[:mine, :], held[mine:, :]
        key = shared.astype(F32)[lead : lead + 1, :]
        tokens = key.shape[1]
        example = lax.broadcasted_iota(jnp.int32, (group_examples, tokens), 0).astype(F32)
        member = (example == key).astype(F32).astype(BF16)
        spread_rows = [member * here[i : i + 1, :] for i in range(mine)]
        spread_rows = jnp.concatenate(
            [jnp.concatenate(spread_rows[i : i + 2], axis=1) for i in range(0, mine, 2)], axis=0
        )
        blank = jnp.zeros_like(err)
        twice = jnp.concatenate(
            [jnp.concatenate([err, blank], axis=1), jnp.concatenate([blank, err], axis=1)], axis=0
        )
        wide.append(
            lax.dot_general(spread_rows, twice, CONTRACT_LAST, preferred_element_type=F32).astype(BF16)
        )
        column = d * rows_here + lax.broadcasted_iota(jnp.int32, (rows_here, tokens), 0)
        shared = shared.astype(F32)
        chosen = shared[:1, :]
        for i in range(1, lead):
            chosen = jnp.where(column >= i * width, shared[i : i + 1, :], chosen)
        product = chosen * picked[:, g * tokens : (g + 1) * tokens]
        upper = product.astype(BF16)
        lower = (product - upper.astype(F32)).astype(BF16)
        part = lax.dot_general(upper, member, CONTRACT_LAST, preferred_element_type=F32)
        part += lax.dot_general(lower, member, CONTRACT_LAST, preferred_element_type=F32)
        narrow.append(part.astype(BF16))
    left = jnp.concatenate(narrow, axis=1)
    blocks = []
    for i in range(mine // 2):
        right = jnp.concatenate(
            [w[i * group_examples : (i + 1) * group_examples, :] for w in wide], axis=0
        )
        blocks.append(jnp.dot(left, right, preferred_element_type=F32))
    out[...] = jnp.concatenate(blocks, axis=1) * scale


def by_tokens(hidden_in, out_grads, piece_of, owner_dp, owner_slot, sketch_in, sketch_out):
    count_dp = lax.axis_size("dp")
    count_fsdp = lax.axis_size("fsdp")
    token_rows = hidden_in.shape[0]
    width = sketch_in.shape[1]
    owned = count_dp // 2
    bits = bits_of(count_fsdp)
    low, top = bits[:-1], bits[-1]
    mine = width // count_fsdp
    lead = -(-GR // width)
    tile = (lead + 8) // 8 * 8
    rows_here = GR // count_dp
    square = jax.ShapeDtypeStruct((width, token_rows), F32)
    own_out, own_in = sketch_out.T, sketch_in.T

    near_out = spread(own_out, low)
    far_out = swap(own_out, "fsdp", top)
    near_in = spread(own_in, low)
    far_in = swap(own_in, "fsdp", top)
    inputs = call(functools.partial(near_kernel, list(range(top))), [*near_in, hidden_in], square)
    out_shards = near_out + spread(after(far_out, inputs), low)
    keys = call(
        functools.partial(keys_kernel, owned),
        [piece_of, owner_dp, owner_slot, inputs],
        jax.ShapeDtypeStruct((16, token_rows), BF16),
        [VMEM, SMEM, SMEM, ANY],
    )
    errors = call(
        functools.partial(errors_kernel, list(range(count_fsdp))),
        [*out_shards, out_grads, inputs, keys],
        jax.ShapeDtypeStruct(square.shape, BF16),
        [VMEM] * (count_fsdp + 1) + [ANY] * 2,
        ERRORS_COST,
    )
    first, *later = bits_of(count_dp)
    order = [0]
    for bit in [*later, first]:
        order += [k ^ bit for k in order]
    half = order[: len(order) // 2]
    errors = jnp.concatenate([errors] + [swap(errors, "dp", k) for k in half[1:]], axis=0)
    far_in = spread(after(far_in, errors), low)
    for k in range(top - 1):
        inputs = call(
            functools.partial(project_kernel, [top + k]), [far_in[k], hidden_in, inputs], square
        )
    messages = call(
        functools.partial(message_kernel, [2 * top - 1], mine, lead),
        [far_in[-1], hidden_in, inputs, keys],
        jax.ShapeDtypeStruct((count_dp * count_fsdp, mine + tile, token_rows), BF16),
    )
    messages = lax.all_to_all(messages, BOTH, split_axis=0, concat_axis=0, tiled=True)
    all_errors = spread(widen(errors, "dp", first), bits)
    picked = call(
        picked_kernel,
        all_errors,
        jax.ShapeDtypeStruct((rows_here, count_dp * count_fsdp * token_rows), F32),
        cost=PICKED_COST,
    )
    scale = 1.0 / math.sqrt(owned * count_dp * count_fsdp)
    return call(
        functools.partial(gram_kernel, order, lead, owned * count_dp, scale),
        [*all_errors, picked, messages],
        jax.ShapeDtypeStruct((rows_here, width * width // count_fsdp), F32),
    )


def by_pieces(hidden_in, out_grads, piece_of, owner_dp, owner_slot, sketch_in, sketch_out):
    count_dp = lax.axis_size("dp")
    count_fsdp = lax.axis_size("fsdp")
    full_in, full_out = (
        lax.all_gather(sketch_in, "fsdp", axis=0, tiled=True),
        lax.all_gather(sketch_out, "fsdp", axis=0, tiled=True),
    )
    inputs_low = jnp.dot(hidden_in, full_in, preferred_element_type=F32).astype(BF16)
    errors_low = jnp.dot(out_grads, full_out, preferred_element_type=F32).astype(BF16)
    rows_here = inputs_low.shape[0]
    width = inputs_low.shape[1]
    pieces = owner_dp.shape[1]
    member = piece_of[0][:, None] == jnp.arange(pieces, dtype=jnp.int32)[None, :]
    spread = (member.astype(BF16)[:, :, None] * inputs_low[:, None, :]).reshape(
        rows_here, pieces * width
    )
    partial_value = lax.dot_general(
        spread, errors_low, (((0,), (0,)), ((), ())), preferred_element_type=F32
    )
    partial_value = partial_value.reshape(pieces, width * width)
    target = owner_dp[0]
    earlier = jnp.arange(pieces)[None, :] < jnp.arange(pieces)[:, None]
    ranked = jnp.sum(((target[:, None] == target[None, :]) & earlier).astype(jnp.int32), axis=1)
    places = target * CAP + ranked
    slots_total = count_dp * CAP
    routing_mask = places[None, :] == jnp.arange(slots_total, dtype=jnp.int32)[:, None]
    outgoing = jnp.dot(routing_mask.astype(F32), partial_value, precision=lax.Precision.HIGHEST)
    labels = jnp.sum(routing_mask.astype(jnp.int32) * (owner_slot[0][None, :] + 1), axis=1) - 1
    incoming, arrived = (
        lax.all_to_all(outgoing, "dp", split_axis=0, concat_axis=0, tiled=True),
        lax.all_to_all(labels, "dp", split_axis=0, concat_axis=0, tiled=True),
    )
    owned = count_dp // 2
    collect = (arrived[None, :] == jnp.arange(owned, dtype=jnp.int32)[:, None]).astype(F32)
    features = jnp.dot(collect, incoming, precision=lax.Precision.HIGHEST).astype(BF16)
    local_gram = lax.dot_general(
        features[:, :GR], features, (((0,), (0,)), ((), ())), preferred_element_type=F32
    )
    scale_factor = 1.0 / math.sqrt(owned * count_dp * count_fsdp)
    section_one = lax.psum_scatter(local_gram, "fsdp", scatter_dimension=1, tiled=True)
    result = lax.psum_scatter(section_one, "dp", scatter_dimension=0, tiled=True)
    return result * scale_factor


def on_device(hidden_in, out_grads, piece_of, owner_dp, owner_slot, sketch_in, sketch_out):
    count_dp = lax.axis_size("dp")
    count_fsdp = lax.axis_size("fsdp")
    token_rows = hidden_in.shape[0]
    width = sketch_in.shape[1]
    gathered = count_dp * count_fsdp * token_rows * 2 * width * 2
    summed = GR * width * width * 4
    doubling = all(n > 1 and n & (n - 1) == 0 for n in (count_dp, count_fsdp))
    whole_tiles = token_rows % 128 == 0 and width % (16 * count_fsdp) == 0
    exact_keys = count_dp * (count_dp // 2) <= 256
    form = by_tokens if gathered <= summed and doubling and whole_tiles and exact_keys else by_pieces
    return form(hidden_in, out_grads, piece_of, owner_dp, owner_slot, sketch_in, sketch_out)


def solution(mesh):
    return jax.shard_map(
        on_device,
        mesh=mesh,
        in_specs=(
            P(("dp", "fsdp"), None),
            P(("dp", "fsdp"), None),
            P(("dp", "fsdp"), None),
            P(("dp", "fsdp"), None),
            P(("dp", "fsdp"), None),
            P("fsdp", None),
            P("fsdp", None),
        ),
        out_specs=P("dp", "fsdp"),
        check_vma=False,
    )
```

```python
import functools
import math

import jax
import jax.numpy as jnp
from jax import lax
from jax.experimental import pallas as pl
from jax.experimental.pallas import tpu as pltpu
from jax.sharding import PartitionSpec as P

CAP = 2
GR = 192
BF16 = jnp.bfloat16
F32 = jnp.float32
BOTH = ("dp", "fsdp")
CONTRACT_LAST = (((1,), (1,)), ((), ()))
VMEM = pl.BlockSpec(memory_space=pltpu.VMEM)
SMEM = pl.BlockSpec(memory_space=pltpu.SMEM)
ANY = pl.BlockSpec(memory_space=pl.ANY)
ERRORS_COST = pl.CostEstimate(
    flops=1_500_000_000, bytes_accessed=1_000_000, transcendentals=0
)
ROOM = pltpu.CompilerParams(vmem_limit_bytes=16 * 1024 * 1024)


def swap(value, axis, bit):
    count = lax.axis_size(axis)
    return lax.ppermute(value, axis, [(i, i ^ bit) for i in range(count)])


def bits_of(count):
    return [1 << k for k in range(count.bit_length() - 1)]


def after(value, *others):
    return lax.optimization_barrier((value, *others))[0]


def widen(rows, axis, bit):
    return jnp.concatenate([rows, swap(rows, axis, bit)], axis=0)


def spread(value, bits):
    held = {0: value}
    for bit in reversed(bits):
        held.update({k ^ bit: swap(v, "fsdp", bit) for k, v in list(held.items())})
    return [held[k] for k in range(len(held))]


def low_rank(sketches, which, tokens):
    me = lax.axis_index("fsdp")
    total = 0.0
    for sketch, k in zip(sketches, which):
        size = sketch.shape[1]
        start = pl.multiple_of((me ^ k) * size, size)
        total += lax.dot_general(
            sketch[...], tokens[:, pl.ds(start, size)], CONTRACT_LAST, preferred_element_type=F32
        )
    return total


def near_kernel(which, *refs):
    refs[-1][...] = low_rank(refs[: len(which)], which, refs[-2])


def project_kernel(which, *refs):
    count = len(which)
    tokens, total, out = refs[count:]
    out[...] = low_rank(refs[:count], which, tokens) + total[...]


def keys_kernel(owned, piece_of, owner_dp, owner_slot, _, out):
    piece = piece_of[...]
    key = jnp.zeros(piece.shape, jnp.int32)
    for p in range(owner_dp.shape[1]):
        key = jnp.where(piece == p, owner_dp[0, p] * owned + owner_slot[0, p], key)
    out[...] = jnp.broadcast_to(key.astype(F32), out.shape).astype(BF16)


def message_kernel(which, mine, lead, *refs):
    count = len(which)
    tokens, total, keys, out = refs[count:]
    rows = (low_rank(refs[:count], which, tokens) + total[...]).astype(BF16)
    shared = jnp.concatenate([rows[:lead, :], keys[: out.shape[1] - mine - lead, :]], axis=0)
    parts = rows.shape[0] // mine
    for k in range(out.shape[0]):
        f = k % parts
        out[k] = jnp.concatenate([rows[f * mine : (f + 1) * mine, :], shared], axis=0)


def call(kernel, operands, outputs, specs=None, cost=None):
    return pl.pallas_call(
        kernel,
        out_shape=outputs,
        in_specs=specs or [VMEM] * len(operands),
        out_specs=VMEM,
        compiler_params=ROOM,
        cost_estimate=cost,
    )(*operands)


def errors_kernel(which, *refs):
    count = len(which)
    refs[-1][...] = low_rank(refs[:count], which, refs[count]).astype(BF16)


def gram_kernel(order, lead, group_examples, scale, *refs):
    errors, messages, out = refs[:-2], refs[-2], refs[-1]
    count_fsdp, count_dp = len(errors), len(order)
    rows_here, columns_here = out.shape
    width = errors[0].shape[0] // count_dp
    mine = columns_here // width
    d, f = lax.axis_index("dp"), lax.axis_index("fsdp")
    wide = []
    for g, e_ref in enumerate(errors):
        places = [(d ^ k) * count_fsdp + (f ^ g) for k in order]
        err = jnp.concatenate([e_ref[k * width : (k + 1) * width, :] for k in range(count_dp)], axis=1)
        low = jnp.concatenate([messages[k] for k in places], axis=1)
        key = low.astype(F32)[mine + lead : mine + lead + 1, :]
        example = lax.broadcasted_iota(jnp.int32, (group_examples, key.shape[1]), 0).astype(F32)
        member = (example == key).astype(F32).astype(BF16)
        rows = [member * low[i : i + 1, :] for i in range(mine + lead + lead % 2)]
        rows = jnp.concatenate(
            [jnp.concatenate(rows[i : i + 2], axis=1) for i in range(0, len(rows), 2)], axis=0
        )
        blank = jnp.zeros_like(err)
        twice = jnp.concatenate(
            [jnp.concatenate([err, blank], axis=1), jnp.concatenate([blank, err], axis=1)], axis=0
        )
        wide.append(
            lax.dot_general(rows, twice, CONTRACT_LAST, preferred_element_type=F32).astype(BF16)
        )

    def pair(i):
        return jnp.concatenate(
            [w[i * group_examples : (i + 1) * group_examples, :] for w in wide], axis=0
        )

    grid = (rows_here, 2 * width)
    column = d * rows_here + lax.broadcasted_iota(jnp.int32, grid, 0)
    at = lax.broadcasted_iota(jnp.int32, grid, 1)
    left = 0.0
    for i in range((lead + 1) // 2):
        pick = (at + 2 * width * i == column).astype(F32).astype(BF16)
        left += lax.dot_general(pick, pair(mine // 2 + i), CONTRACT_LAST, preferred_element_type=F32)
    left = left.astype(BF16)
    blocks = [jnp.dot(left, pair(i), preferred_element_type=F32) for i in range(mine // 2)]
    out[...] = jnp.concatenate(blocks, axis=1) * scale


def by_tokens(hidden_in, out_grads, piece_of, owner_dp, owner_slot, sketch_in, sketch_out):
    count_dp = lax.axis_size("dp")
    count_fsdp = lax.axis_size("fsdp")
    token_rows = hidden_in.shape[0]
    width = sketch_in.shape[1]
    owned = count_dp // 2
    bits = bits_of(count_fsdp)
    low, top = bits[:-1], bits[-1]
    mine = width // count_fsdp
    lead = -(-GR // width)
    tile = (lead + 8) // 8 * 8
    rows_here = GR // count_dp
    square = jax.ShapeDtypeStruct((width, token_rows), F32)
    own_out, own_in = sketch_out.T, sketch_in.T

    near_out = spread(own_out, low)
    far_out = swap(own_out, "fsdp", top)
    near_in = spread(own_in, low)
    far_in = swap(own_in, "fsdp", top)
    inputs = call(functools.partial(near_kernel, list(range(top))), [*near_in, hidden_in], square)
    out_shards = near_out + spread(after(far_out, inputs), low)
    keys = call(
        functools.partial(keys_kernel, owned),
        [piece_of, owner_dp, owner_slot, inputs],
        jax.ShapeDtypeStruct((16, token_rows), BF16),
        [VMEM, SMEM, SMEM, ANY],
    )
    errors = call(
        functools.partial(errors_kernel, list(range(count_fsdp))),
        [*out_shards, out_grads, inputs, keys],
        jax.ShapeDtypeStruct(square.shape, BF16),
        [VMEM] * (count_fsdp + 1) + [ANY] * 2,
        ERRORS_COST,
    )
    first, *later = bits_of(count_dp)
    order = [0]
    for bit in [*later, first]:
        order += [k ^ bit for k in order]
    half = order[: len(order) // 2]
    errors = jnp.concatenate([errors] + [swap(errors, "dp", k) for k in half[1:]], axis=0)
    far_in = spread(after(far_in, errors), low)
    for k in range(top - 1):
        inputs = call(
            functools.partial(project_kernel, [top + k]), [far_in[k], hidden_in, inputs], square
        )
    messages = call(
        functools.partial(message_kernel, [2 * top - 1], mine, lead),
        [far_in[-1], hidden_in, inputs, keys],
        jax.ShapeDtypeStruct((count_dp * count_fsdp, mine + tile, token_rows), BF16),
    )
    messages = lax.all_to_all(messages, BOTH, split_axis=0, concat_axis=0, tiled=True)
    all_errors = spread(widen(errors, "dp", first), bits)
    scale = 1.0 / math.sqrt(owned * count_dp * count_fsdp)
    return call(
        functools.partial(gram_kernel, order, lead, owned * count_dp, scale),
        [*all_errors, messages],
        jax.ShapeDtypeStruct((rows_here, width * width // count_fsdp), F32),
    )


def by_pieces(hidden_in, out_grads, piece_of, owner_dp, owner_slot, sketch_in, sketch_out):
    count_dp = lax.axis_size("dp")
    count_fsdp = lax.axis_size("fsdp")
    full_in, full_out = (
        lax.all_gather(sketch_in, "fsdp", axis=0, tiled=True),
        lax.all_gather(sketch_out, "fsdp", axis=0, tiled=True),
    )
    inputs_low = jnp.dot(hidden_in, full_in, preferred_element_type=F32).astype(BF16)
    errors_low = jnp.dot(out_grads, full_out, preferred_element_type=F32).astype(BF16)
    rows_here = inputs_low.shape[0]
    width = inputs_low.shape[1]
    pieces = owner_dp.shape[1]
    member = piece_of[0][:, None] == jnp.arange(pieces, dtype=jnp.int32)[None, :]
    spread = (member.astype(BF16)[:, :, None] * inputs_low[:, None, :]).reshape(
        rows_here, pieces * width
    )
    partial_value = lax.dot_general(
        spread, errors_low, (((0,), (0,)), ((), ())), preferred_element_type=F32
    )
    partial_value = partial_value.reshape(pieces, width * width)
    target = owner_dp[0]
    earlier = jnp.arange(pieces)[None, :] < jnp.arange(pieces)[:, None]
    ranked = jnp.sum(((target[:, None] == target[None, :]) & earlier).astype(jnp.int32), axis=1)
    places = target * CAP + ranked
    slots_total = count_dp * CAP
    routing_mask = places[None, :] == jnp.arange(slots_total, dtype=jnp.int32)[:, None]
    outgoing = jnp.dot(routing_mask.astype(F32), partial_value, precision=lax.Precision.HIGHEST)
    labels = jnp.sum(routing_mask.astype(jnp.int32) * (owner_slot[0][None, :] + 1), axis=1) - 1
    incoming, arrived = (
        lax.all_to_all(outgoing, "dp", split_axis=0, concat_axis=0, tiled=True),
        lax.all_to_all(labels, "dp", split_axis=0, concat_axis=0, tiled=True),
    )
    owned = count_dp // 2
    collect = (arrived[None, :] == jnp.arange(owned, dtype=jnp.int32)[:, None]).astype(F32)
    features = jnp.dot(collect, incoming, precision=lax.Precision.HIGHEST).astype(BF16)
    local_gram = lax.dot_general(
        features[:, :GR], features, (((0,), (0,)), ((), ())), preferred_element_type=F32
    )
    scale_factor = 1.0 / math.sqrt(owned * count_dp * count_fsdp)
    section_one = lax.psum_scatter(local_gram, "fsdp", scatter_dimension=1, tiled=True)
    result = lax.psum_scatter(section_one, "dp", scatter_dimension=0, tiled=True)
    return result * scale_factor


def on_device(hidden_in, out_grads, piece_of, owner_dp, owner_slot, sketch_in, sketch_out):
    count_dp = lax.axis_size("dp")
    count_fsdp = lax.axis_size("fsdp")
    token_rows = hidden_in.shape[0]
    width = sketch_in.shape[1]
    gathered = count_dp * count_fsdp * token_rows * 2 * width * 2
    summed = GR * width * width * 4
    doubling = all(n > 1 and n & (n - 1) == 0 for n in (count_dp, count_fsdp))
    whole_tiles = token_rows % 128 == 0 and width % (16 * count_fsdp) == 0
    exact_keys = count_dp * (count_dp // 2) <= 256
    form = by_tokens if gathered <= summed and doubling and whole_tiles and exact_keys else by_pieces
    return form(hidden_in, out_grads, piece_of, owner_dp, owner_slot, sketch_in, sketch_out)


def solution(mesh):
    return jax.shard_map(
        on_device,
        mesh=mesh,
        in_specs=(
            P(("dp", "fsdp"), None),
            P(("dp", "fsdp"), None),
            P(("dp", "fsdp"), None),
            P(("dp", "fsdp"), None),
            P(("dp", "fsdp"), None),
            P("fsdp", None),
            P("fsdp", None),
        ),
        out_specs=P("dp", "fsdp"),
        check_vma=False,
    )
```

```python
import functools
import math

import jax
import jax.numpy as jnp
from jax import lax
from jax.experimental import pallas as pl
from jax.experimental.pallas import tpu as pltpu
from jax.sharding import PartitionSpec as P

CAP = 2
GR = 192
BF16 = jnp.bfloat16
F32 = jnp.float32
CONTRACT_LAST = (((1,), (1,)), ((), ()))
VMEM = pl.BlockSpec(memory_space=pltpu.VMEM)
SMEM = pl.BlockSpec(memory_space=pltpu.SMEM)
ANY = pl.BlockSpec(memory_space=pl.ANY)
ERRORS_COST = pl.CostEstimate(
    flops=1_500_000_000, bytes_accessed=1_000_000, transcendentals=0
)
ROOM = pltpu.CompilerParams(vmem_limit_bytes=16 * 1024 * 1024)


def swap(value, axis, bit):
    count = lax.axis_size(axis)
    return lax.ppermute(value, axis, [(i, i ^ bit) for i in range(count)])


def bits_of(count):
    return [1 << k for k in range(count.bit_length() - 1)]


def after(value, *others):
    return lax.optimization_barrier((value, *others))[0]


def widen(rows, axis, bit):
    return jnp.concatenate([rows, swap(rows, axis, bit)], axis=0)


def spread(value, bits):
    held = {0: value}
    for bit in reversed(bits):
        held.update({k ^ bit: swap(v, "fsdp", bit) for k, v in list(held.items())})
    return [held[k] for k in range(len(held))]


def low_rank(sketches, which, tokens):
    me = lax.axis_index("fsdp")
    total = 0.0
    for sketch, k in zip(sketches, which):
        size = sketch.shape[1]
        start = pl.multiple_of((me ^ k) * size, size)
        total += lax.dot_general(
            sketch[...], tokens[:, pl.ds(start, size)], CONTRACT_LAST, preferred_element_type=F32
        )
    return total


def near_kernel(which, *refs):
    refs[-1][...] = low_rank(refs[: len(which)], which, refs[-2])


def project_kernel(which, *refs):
    count = len(which)
    tokens, total, out = refs[count:]
    out[...] = low_rank(refs[:count], which, tokens) + total[...]


def keys_kernel(owned, piece_of, owner_dp, owner_slot, _, out):
    piece = piece_of[...]
    key = jnp.zeros(piece.shape, jnp.int32)
    for p in range(owner_dp.shape[1]):
        key = jnp.where(piece == p, owner_dp[0, p] * owned + owner_slot[0, p], key)
    out[...] = jnp.broadcast_to(key.astype(F32), out.shape).astype(BF16)


def message_kernel(which, mine, lead, *refs):
    count = len(which)
    tokens, total, keys, out = refs[count:]
    rows = (low_rank(refs[:count], which, tokens) + total[...]).astype(BF16)
    shared = jnp.concatenate([rows[:lead, :], keys[: out.shape[1] - mine - lead, :]], axis=0)
    each = out.shape[0] * mine // rows.shape[0]
    for k in range(out.shape[0]):
        f = k // each
        out[k] = jnp.concatenate([rows[f * mine : (f + 1) * mine, :], shared], axis=0)


def call(kernel, operands, outputs, specs=None, cost=None):
    return pl.pallas_call(
        kernel,
        out_shape=outputs,
        in_specs=specs or [VMEM] * len(operands),
        out_specs=VMEM,
        compiler_params=ROOM,
        cost_estimate=cost,
    )(*operands)


def errors_kernel(which, *refs):
    count = len(which)
    refs[-1][...] = low_rank(refs[:count], which, refs[count]).astype(BF16)


def gram_kernel(order, lead, group_examples, scale, *refs):
    errors, messages, out = refs[:-2], refs[-2], refs[-1]
    count_fsdp, count_dp = len(errors), len(order)
    rows_here, columns_here = out.shape
    width = errors[0].shape[0] // count_dp
    mine = columns_here // width
    d, f = lax.axis_index("dp"), lax.axis_index("fsdp")
    wide = []
    for g, e_ref in enumerate(errors):
        places = [(f ^ g) * count_dp + (d ^ k) for k in order]
        err = jnp.concatenate([e_ref[k * width : (k + 1) * width, :] for k in range(count_dp)], axis=1)
        low = jnp.concatenate([messages[k] for k in places], axis=1)
        key = low.astype(F32)[mine + lead : mine + lead + 1, :]
        example = lax.broadcasted_iota(jnp.int32, (group_examples, key.shape[1]), 0).astype(F32)
        member = (example == key).astype(F32).astype(BF16)
        rows = [member * low[i : i + 1, :] for i in range(mine + lead + lead % 2)]
        rows = jnp.concatenate(
            [jnp.concatenate(rows[i : i + 2], axis=1) for i in range(0, len(rows), 2)], axis=0
        )
        blank = jnp.zeros_like(err)
        twice = jnp.concatenate(
            [jnp.concatenate([err, blank], axis=1), jnp.concatenate([blank, err], axis=1)], axis=0
        )
        wide.append(
            lax.dot_general(rows, twice, CONTRACT_LAST, preferred_element_type=F32).astype(BF16)
        )

    def pair(i):
        return jnp.concatenate(
            [w[i * group_examples : (i + 1) * group_examples, :] for w in wide], axis=0
        )

    grid = (rows_here, 2 * width)
    column = d * rows_here + lax.broadcasted_iota(jnp.int32, grid, 0)
    at = lax.broadcasted_iota(jnp.int32, grid, 1)
    left = 0.0
    for i in range((lead + 1) // 2):
        pick = (at + 2 * width * i == column).astype(F32).astype(BF16)
        left += lax.dot_general(pick, pair(mine // 2 + i), CONTRACT_LAST, preferred_element_type=F32)
    left = left.astype(BF16)
    blocks = [jnp.dot(left, pair(i), preferred_element_type=F32) for i in range(mine // 2)]
    out[...] = jnp.concatenate(blocks, axis=1) * scale


def by_tokens(hidden_in, out_grads, piece_of, owner_dp, owner_slot, sketch_in, sketch_out):
    count_dp = lax.axis_size("dp")
    count_fsdp = lax.axis_size("fsdp")
    token_rows = hidden_in.shape[0]
    width = sketch_in.shape[1]
    owned = count_dp // 2
    bits = bits_of(count_fsdp)
    low, top = bits[:-1], bits[-1]
    mine = width // count_fsdp
    lead = -(-GR // width)
    tile = (lead + 8) // 8 * 8
    rows_here = GR // count_dp
    square = jax.ShapeDtypeStruct((width, token_rows), F32)
    own_out, own_in = sketch_out.T, sketch_in.T

    near_out = spread(own_out, low)
    far_out = swap(own_out, "fsdp", top)
    near_in = spread(own_in, low)
    far_in = swap(own_in, "fsdp", top)
    inputs = call(functools.partial(near_kernel, list(range(top))), [*near_in, hidden_in], square)
    out_shards = near_out + spread(after(far_out, inputs), low)
    keys = call(
        functools.partial(keys_kernel, owned),
        [piece_of, owner_dp, owner_slot, inputs],
        jax.ShapeDtypeStruct((16, token_rows), BF16),
        [VMEM, SMEM, SMEM, ANY],
    )
    errors = call(
        functools.partial(errors_kernel, list(range(count_fsdp))),
        [*out_shards, out_grads, inputs, keys],
        jax.ShapeDtypeStruct(square.shape, BF16),
        [VMEM] * (count_fsdp + 1) + [ANY] * 2,
        ERRORS_COST,
    )
    first, *later = bits_of(count_dp)
    order = [0]
    for bit in [*later, first]:
        order += [k ^ bit for k in order]
    half = order[: len(order) // 2]
    errors = jnp.concatenate([errors] + [swap(errors, "dp", k) for k in half[1:]], axis=0)
    far_in = spread(after(far_in, errors), low)
    for k in range(top - 1):
        inputs = call(
            functools.partial(project_kernel, [top + k]), [far_in[k], hidden_in, inputs], square
        )
    messages = call(
        functools.partial(message_kernel, [2 * top - 1], mine, lead),
        [far_in[-1], hidden_in, inputs, keys],
        jax.ShapeDtypeStruct((count_dp * count_fsdp, mine + tile, token_rows), BF16),
    )
    messages = lax.all_to_all(messages, ("fsdp", "dp"), split_axis=0, concat_axis=0, tiled=True)
    all_errors = spread(widen(errors, "dp", first), bits)
    scale = 1.0 / math.sqrt(owned * count_dp * count_fsdp)
    return call(
        functools.partial(gram_kernel, order, lead, owned * count_dp, scale),
        [*all_errors, messages],
        jax.ShapeDtypeStruct((rows_here, width * width // count_fsdp), F32),
    )


def by_pieces(hidden_in, out_grads, piece_of, owner_dp, owner_slot, sketch_in, sketch_out):
    count_dp = lax.axis_size("dp")
    count_fsdp = lax.axis_size("fsdp")
    full_in, full_out = (
        lax.all_gather(sketch_in, "fsdp", axis=0, tiled=True),
        lax.all_gather(sketch_out, "fsdp", axis=0, tiled=True),
    )
    inputs_low = jnp.dot(hidden_in, full_in, preferred_element_type=F32).astype(BF16)
    errors_low = jnp.dot(out_grads, full_out, preferred_element_type=F32).astype(BF16)
    rows_here = inputs_low.shape[0]
    width = inputs_low.shape[1]
    pieces = owner_dp.shape[1]
    member = piece_of[0][:, None] == jnp.arange(pieces, dtype=jnp.int32)[None, :]
    spread = (member.astype(BF16)[:, :, None] * inputs_low[:, None, :]).reshape(
        rows_here, pieces * width
    )
    partial_value = lax.dot_general(
        spread, errors_low, (((0,), (0,)), ((), ())), preferred_element_type=F32
    )
    partial_value = partial_value.reshape(pieces, width * width)
    target = owner_dp[0]
    earlier = jnp.arange(pieces)[None, :] < jnp.arange(pieces)[:, None]
    ranked = jnp.sum(((target[:, None] == target[None, :]) & earlier).astype(jnp.int32), axis=1)
    places = target * CAP + ranked
    slots_total = count_dp * CAP
    routing_mask = places[None, :] == jnp.arange(slots_total, dtype=jnp.int32)[:, None]
    outgoing = jnp.dot(routing_mask.astype(F32), partial_value, precision=lax.Precision.HIGHEST)
    labels = jnp.sum(routing_mask.astype(jnp.int32) * (owner_slot[0][None, :] + 1), axis=1) - 1
    incoming, arrived = (
        lax.all_to_all(outgoing, "dp", split_axis=0, concat_axis=0, tiled=True),
        lax.all_to_all(labels, "dp", split_axis=0, concat_axis=0, tiled=True),
    )
    owned = count_dp // 2
    collect = (arrived[None, :] == jnp.arange(owned, dtype=jnp.int32)[:, None]).astype(F32)
    features = jnp.dot(collect, incoming, precision=lax.Precision.HIGHEST).astype(BF16)
    local_gram = lax.dot_general(
        features[:, :GR], features, (((0,), (0,)), ((), ())), preferred_element_type=F32
    )
    scale_factor = 1.0 / math.sqrt(owned * count_dp * count_fsdp)
    section_one = lax.psum_scatter(local_gram, "fsdp", scatter_dimension=1, tiled=True)
    result = lax.psum_scatter(section_one, "dp", scatter_dimension=0, tiled=True)
    return result * scale_factor


def on_device(hidden_in, out_grads, piece_of, owner_dp, owner_slot, sketch_in, sketch_out):
    count_dp = lax.axis_size("dp")
    count_fsdp = lax.axis_size("fsdp")
    token_rows = hidden_in.shape[0]
    width = sketch_in.shape[1]
    gathered = count_dp * count_fsdp * token_rows * 2 * width * 2
    summed = GR * width * width * 4
    doubling = all(n > 1 and n & (n - 1) == 0 for n in (count_dp, count_fsdp))
    whole_tiles = token_rows % 128 == 0 and width % (16 * count_fsdp) == 0
    exact_keys = count_dp * (count_dp // 2) <= 256
    form = by_tokens if gathered <= summed and doubling and whole_tiles and exact_keys else by_pieces
    return form(hidden_in, out_grads, piece_of, owner_dp, owner_slot, sketch_in, sketch_out)


def solution(mesh):
    return jax.shard_map(
        on_device,
        mesh=mesh,
        in_specs=(
            P(("dp", "fsdp"), None),
            P(("dp", "fsdp"), None),
            P(("dp", "fsdp"), None),
            P(("dp", "fsdp"), None),
            P(("dp", "fsdp"), None),
            P("fsdp", None),
            P("fsdp", None),
        ),
        out_specs=P("dp", "fsdp"),
        check_vma=False,
    )
```

```python
import functools
import math

import jax
import jax.numpy as jnp
from jax import lax
from jax.experimental import pallas as pl
from jax.experimental.pallas import tpu as pltpu
from jax.sharding import PartitionSpec as P

CAP = 2
GR = 192
BF16 = jnp.bfloat16
F32 = jnp.float32
CONTRACT_LAST = (((1,), (1,)), ((), ()))
VMEM = pl.BlockSpec(memory_space=pltpu.VMEM)
SMEM = pl.BlockSpec(memory_space=pltpu.SMEM)
ANY = pl.BlockSpec(memory_space=pl.ANY)
ERRORS_COST = pl.CostEstimate(
    flops=1_500_000_000, bytes_accessed=1_000_000, transcendentals=0
)
ROOM = pltpu.CompilerParams(vmem_limit_bytes=16 * 1024 * 1024)


def swap(value, axis, bit):
    count = lax.axis_size(axis)
    return lax.ppermute(value, axis, [(i, i ^ bit) for i in range(count)])


def bits_of(count):
    return [1 << k for k in range(count.bit_length() - 1)]


def after(value, *others):
    return lax.optimization_barrier((value, *others))[0]


def widen(rows, axis, bit):
    return jnp.concatenate([rows, swap(rows, axis, bit)], axis=0)


def spread(value, bits):
    held = {0: value}
    for bit in reversed(bits):
        held.update({k ^ bit: swap(v, "fsdp", bit) for k, v in list(held.items())})
    return [held[k] for k in range(len(held))]


def low_rank(sketches, which, tokens):
    me = lax.axis_index("fsdp")
    total = 0.0
    for sketch, k in zip(sketches, which):
        size = sketch.shape[1]
        start = pl.multiple_of((me ^ k) * size, size)
        total += lax.dot_general(
            sketch[...], tokens[:, pl.ds(start, size)], CONTRACT_LAST, preferred_element_type=F32
        )
    return total


def near_kernel(which, *refs):
    refs[-1][...] = low_rank(refs[: len(which)], which, refs[-2])


def keys_kernel(owned, piece_of, owner_dp, owner_slot, _, out):
    piece = piece_of[...]
    key = jnp.zeros(piece.shape, jnp.int32)
    for p in range(owner_dp.shape[1]):
        key = jnp.where(piece == p, owner_dp[0, p] * owned + owner_slot[0, p], key)
    out[...] = jnp.broadcast_to(key.astype(F32), out.shape).astype(BF16)


def message_kernel(which, mine, lead, *refs):
    count = len(which)
    tokens, total, keys, out = refs[count:]
    rows = (low_rank(refs[:count], which, tokens) + total[...]).astype(BF16)
    shared = jnp.concatenate([rows[:lead, :], keys[: out.shape[1] - mine - lead, :]], axis=0)
    each = out.shape[0] * mine // rows.shape[0]
    for k in range(out.shape[0]):
        f = k // each
        out[k] = jnp.concatenate([rows[f * mine : (f + 1) * mine, :], shared], axis=0)


def call(kernel, operands, outputs, specs=None, cost=None):
    return pl.pallas_call(
        kernel,
        out_shape=outputs,
        in_specs=specs or [VMEM] * len(operands),
        out_specs=VMEM,
        compiler_params=ROOM,
        cost_estimate=cost,
    )(*operands)


def errors_kernel(which, *refs):
    count = len(which)
    refs[-1][...] = low_rank(refs[:count], which, refs[count]).astype(BF16)


def gram_kernel(order, lead, group_examples, scale, *refs):
    errors, messages, out = refs[:-2], refs[-2], refs[-1]
    count_fsdp, count_dp = len(errors), len(order)
    rows_here, columns_here = out.shape
    width = errors[0].shape[0] // count_dp
    mine = columns_here // width
    d, f = lax.axis_index("dp"), lax.axis_index("fsdp")
    wide = []
    for g, e_ref in enumerate(errors):
        places = [(f ^ g) * count_dp + (d ^ k) for k in order]
        err = jnp.concatenate([e_ref[k * width : (k + 1) * width, :] for k in range(count_dp)], axis=1)
        low = jnp.concatenate([messages[k] for k in places], axis=1)
        key = low.astype(F32)[mine + lead : mine + lead + 1, :]
        example = lax.broadcasted_iota(jnp.int32, (group_examples, key.shape[1]), 0).astype(F32)
        member = (example == key).astype(F32).astype(BF16)
        rows = [member * low[i : i + 1, :] for i in range(mine + lead + lead % 2)]
        rows = jnp.concatenate(
            [jnp.concatenate(rows[i : i + 2], axis=1) for i in range(0, len(rows), 2)], axis=0
        )
        blank = jnp.zeros_like(err)
        twice = jnp.concatenate(
            [jnp.concatenate([err, blank], axis=1), jnp.concatenate([blank, err], axis=1)], axis=0
        )
        wide.append(
            lax.dot_general(rows, twice, CONTRACT_LAST, preferred_element_type=F32).astype(BF16)
        )

    def pair(i):
        return jnp.concatenate(
            [w[i * group_examples : (i + 1) * group_examples, :] for w in wide], axis=0
        )

    grid = (rows_here, 2 * width)
    column = d * rows_here + lax.broadcasted_iota(jnp.int32, grid, 0)
    at = lax.broadcasted_iota(jnp.int32, grid, 1)
    left = 0.0
    for i in range((lead + 1) // 2):
        pick = (at + 2 * width * i == column).astype(F32).astype(BF16)
        left += lax.dot_general(pick, pair(mine // 2 + i), CONTRACT_LAST, preferred_element_type=F32)
    left = left.astype(BF16)
    blocks = [jnp.dot(left, pair(i), preferred_element_type=F32) for i in range(mine // 2)]
    out[...] = jnp.concatenate(blocks, axis=1) * scale


def by_tokens(hidden_in, out_grads, piece_of, owner_dp, owner_slot, sketch_in, sketch_out):
    count_dp = lax.axis_size("dp")
    count_fsdp = lax.axis_size("fsdp")
    token_rows = hidden_in.shape[0]
    width = sketch_in.shape[1]
    owned = count_dp // 2
    bits = bits_of(count_fsdp)
    low, top = bits[:-1], bits[-1]
    mine = width // count_fsdp
    lead = -(-GR // width)
    tile = (lead + 8) // 8 * 8
    rows_here = GR // count_dp
    square = jax.ShapeDtypeStruct((width, token_rows), F32)
    own_out, own_in = sketch_out.T, sketch_in.T

    near_out = spread(own_out, low)
    far_out = swap(own_out, "fsdp", top)
    near_in = spread(own_in, low)
    far_in = swap(own_in, "fsdp", top)
    inputs = call(functools.partial(near_kernel, list(range(top))), [*near_in, hidden_in], square)
    out_shards = near_out + spread(after(far_out, inputs), low)
    keys = call(
        functools.partial(keys_kernel, owned),
        [piece_of, owner_dp, owner_slot, inputs],
        jax.ShapeDtypeStruct((16, token_rows), BF16),
        [VMEM, SMEM, SMEM, ANY],
    )
    errors = call(
        functools.partial(errors_kernel, list(range(count_fsdp))),
        [*out_shards, out_grads, inputs, keys],
        jax.ShapeDtypeStruct(square.shape, BF16),
        [VMEM] * (count_fsdp + 1) + [ANY] * 2,
        ERRORS_COST,
    )
    first, *later = bits_of(count_dp)
    order = [0]
    for bit in [*later, first]:
        order += [k ^ bit for k in order]
    half = order[: len(order) // 2]
    errors = jnp.concatenate([errors] + [swap(errors, "dp", k) for k in half[1:]], axis=0)
    far_in = spread(after(far_in, errors), low)
    messages = call(
        functools.partial(message_kernel, list(range(top, 2 * top)), mine, lead),
        [*far_in, hidden_in, inputs, keys],
        jax.ShapeDtypeStruct((count_dp * count_fsdp, mine + tile, token_rows), BF16),
    )
    messages = lax.all_to_all(messages, ("fsdp", "dp"), split_axis=0, concat_axis=0, tiled=True)
    all_errors = spread(widen(errors, "dp", first), bits)
    scale = 1.0 / math.sqrt(owned * count_dp * count_fsdp)
    return call(
        functools.partial(gram_kernel, order, lead, owned * count_dp, scale),
        [*all_errors, messages],
        jax.ShapeDtypeStruct((rows_here, width * width // count_fsdp), F32),
    )


def by_pieces(hidden_in, out_grads, piece_of, owner_dp, owner_slot, sketch_in, sketch_out):
    count_dp = lax.axis_size("dp")
    count_fsdp = lax.axis_size("fsdp")
    full_in, full_out = (
        lax.all_gather(sketch_in, "fsdp", axis=0, tiled=True),
        lax.all_gather(sketch_out, "fsdp", axis=0, tiled=True),
    )
    inputs_low = jnp.dot(hidden_in, full_in, preferred_element_type=F32).astype(BF16)
    errors_low = jnp.dot(out_grads, full_out, preferred_element_type=F32).astype(BF16)
    rows_here = inputs_low.shape[0]
    width = inputs_low.shape[1]
    pieces = owner_dp.shape[1]
    member = piece_of[0][:, None] == jnp.arange(pieces, dtype=jnp.int32)[None, :]
    spread = (member.astype(BF16)[:, :, None] * inputs_low[:, None, :]).reshape(
        rows_here, pieces * width
    )
    partial_value = lax.dot_general(
        spread, errors_low, (((0,), (0,)), ((), ())), preferred_element_type=F32
    )
    partial_value = partial_value.reshape(pieces, width * width)
    target = owner_dp[0]
    earlier = jnp.arange(pieces)[None, :] < jnp.arange(pieces)[:, None]
    ranked = jnp.sum(((target[:, None] == target[None, :]) & earlier).astype(jnp.int32), axis=1)
    places = target * CAP + ranked
    slots_total = count_dp * CAP
    routing_mask = places[None, :] == jnp.arange(slots_total, dtype=jnp.int32)[:, None]
    outgoing = jnp.dot(routing_mask.astype(F32), partial_value, precision=lax.Precision.HIGHEST)
    labels = jnp.sum(routing_mask.astype(jnp.int32) * (owner_slot[0][None, :] + 1), axis=1) - 1
    incoming, arrived = (
        lax.all_to_all(outgoing, "dp", split_axis=0, concat_axis=0, tiled=True),
        lax.all_to_all(labels, "dp", split_axis=0, concat_axis=0, tiled=True),
    )
    owned = count_dp // 2
    collect = (arrived[None, :] == jnp.arange(owned, dtype=jnp.int32)[:, None]).astype(F32)
    features = jnp.dot(collect, incoming, precision=lax.Precision.HIGHEST).astype(BF16)
    local_gram = lax.dot_general(
        features[:, :GR], features, (((0,), (0,)), ((), ())), preferred_element_type=F32
    )
    scale_factor = 1.0 / math.sqrt(owned * count_dp * count_fsdp)
    section_one = lax.psum_scatter(local_gram, "fsdp", scatter_dimension=1, tiled=True)
    result = lax.psum_scatter(section_one, "dp", scatter_dimension=0, tiled=True)
    return result * scale_factor


def on_device(hidden_in, out_grads, piece_of, owner_dp, owner_slot, sketch_in, sketch_out):
    count_dp = lax.axis_size("dp")
    count_fsdp = lax.axis_size("fsdp")
    token_rows = hidden_in.shape[0]
    width = sketch_in.shape[1]
    gathered = count_dp * count_fsdp * token_rows * 2 * width * 2
    summed = GR * width * width * 4
    doubling = all(n > 1 and n & (n - 1) == 0 for n in (count_dp, count_fsdp))
    whole_tiles = token_rows % 128 == 0 and width % (16 * count_fsdp) == 0
    exact_keys = count_dp * (count_dp // 2) <= 256
    form = by_tokens if gathered <= summed and doubling and whole_tiles and exact_keys else by_pieces
    return form(hidden_in, out_grads, piece_of, owner_dp, owner_slot, sketch_in, sketch_out)


def solution(mesh):
    return jax.shard_map(
        on_device,
        mesh=mesh,
        in_specs=(
            P(("dp", "fsdp"), None),
            P(("dp", "fsdp"), None),
            P(("dp", "fsdp"), None),
            P(("dp", "fsdp"), None),
            P(("dp", "fsdp"), None),
            P("fsdp", None),
            P("fsdp", None),
        ),
        out_specs=P("dp", "fsdp"),
        check_vma=False,
    )
```
